128 devices in a mesh: row: 8 (over z, core), col: 16 (over x, y).
Axes of the slice: x: 4, y: 4, z: 4, core: 2. Of those that a mesh axis runs over, the one named last changes fastest.
Arguments:
- panel: float32 [2, 16, 1024, 8, 1024], P(None, 'col', None, 'row'), may hold values from -0.03125 to 0.03125
- right_side: float32 [2, 16, 1024, 256], P(None, 'col'), may hold values from -6 to 6
- inverse_blocks: float32 [8, 1024, 1024], P('row'), may hold values from -0.5 to 1.7, as said below
Outputs:
- solved: float32 [8, 1024, 256], P('row')
- updated: float32 [2, 16, 1024, 256], P(None, 'col', 'row')
The draws below stay inside these ranges and needn't reach their ends.
Inputs may be any that keep to these rules, and one draw needn't show every extreme that they name: `inverse_blocks`: each block is invertible and of order one.
All inputs are finite; a program needn't handle non-finite values.
Results may differ from the reference program's by a relative error of at most 0.0001.
Values sent between devices are 32-bit elements; how exact they have to be, the bound alone decides.
No kernel may reach another device: no remote copies, remote signals or barrier semaphores. Data moves between devices by JAX's collectives and lax.ppermute only.
A program may use at most 128 MiB of HBM per device.

```python
import jax
import jax.numpy as jnp
from jax import lax

BS = 1024
RB = 2
R = 256
N = 32768
N_ROW = 8
N_COL = 16


def draw_inverse_blocks(key, part):
    key = jax.random.fold_in(key, 7)
    key_noise, key_diag = jax.random.split(key)
    spread = 0.4 / BS ** 0.5
    noise = jnp.clip(jax.random.normal(key_noise, (N_ROW, BS, BS), jnp.float32), -4.0, 4.0) * spread
    diag = jax.random.uniform(key_diag, (N_ROW, BS), jnp.float32, 0.8, 1.2)
    eye = jnp.eye(BS, dtype=jnp.float32)
    return noise + eye[None, :, :] * diag[:, :, None]


def level_of(key, dims, cuts, low, top_value):
    def one(position, shards_of):
        steps = jax.random.uniform(jax.random.fold_in(jax.random.fold_in(key, 6), position), (shards_of,), jnp.float32, low / len(cuts), top_value / len(cuts))
        return jnp.repeat(jnp.exp(steps), dims[position] // shards_of).reshape((-1,) + (1,) * (len(dims) - position - 1))

    level = one(*cuts[0])
    for cut in cuts[1:]:
        level = level * one(*cut)
    return level


def normal_values(rng, dims, scale, reach, shards=(), kind=jnp.bfloat16):
    drawn = scale * jax.random.normal(rng, dims, jnp.float32)
    if shards:
        drawn = drawn * level_of(rng, dims, shards, -0.22, 0.18)
    return jnp.clip(drawn, -reach, reach).astype(kind)


def setup_inputs(seed: int = 0) -> dict:
    key_of = jax.random.split(jax.random.key(seed), 4)
    panel = normal_values(key_of[0], (RB, N_COL, BS, N_ROW, BS), N ** -0.5, 0.03125, ((1, 16), (3, 8)), jnp.float32)
    right_side = normal_values(key_of[1], (RB, N_COL, BS, R), 1.0, 6.0, ((1, 16),), jnp.float32)
    inverse_blocks = draw_inverse_blocks(jax.random.fold_in(key_of[3], 71), 0)
    return {"panel": panel, "right_side": right_side, "inverse_blocks": inverse_blocks}


def reference(panel, right_side, inverse_blocks):
    highest = lax.Precision.HIGHEST
    blocks = jnp.arange(RB)[:, None] * N_COL + jnp.arange(N_COL)[None, :]
    solved = []
    for k in range(N_ROW):
        rhs = right_side[0, k]
        for r in range(k):
            rhs = rhs - jnp.dot(panel[0, k, :, r, :], solved[r], precision=highest)
        solved.append(jnp.dot(inverse_blocks[k], rhs, precision=highest))
    updated = right_side
    for r in range(N_ROW):
        keep = (blocks > r).astype(jnp.float32)[:, :, None, None]
        term = jnp.einsum("acij,jn->acin", panel[:, :, :, r, :], solved[r], precision=highest)
        updated = updated - keep * term
    return jnp.stack(solved), updated
```

```python
import functools

import jax
import jax.numpy as jnp
from jax import lax
from jax.experimental import pallas as pl
from jax.experimental.pallas import tpu as pltpu
from jax.sharding import PartitionSpec as P

F32 = jnp.float32
BF16 = jnp.bfloat16
LIMIT = 48 * 1024 * 1024
BOTH = ("row", "col")


def halves(x):
    hi = x.astype(BF16)
    return hi, (x - hi.astype(F32)).astype(BF16)


def joined(x):
    return jnp.concatenate(halves(x), axis=1)


def product(w, cat):
    width = cat.shape[1] // 2
    one = jnp.dot(w[0], cat, preferred_element_type=F32)
    two = jnp.dot(w[1], cat[:, :width], preferred_element_type=F32)
    return one[:, :width] + one[:, width:] + two


def cost(flops, nbytes):
    return pl.CostEstimate(flops=flops, bytes_accessed=nbytes, transcendentals=0)


def params():
    return pltpu.CompilerParams(vmem_limit_bytes=LIMIT)


def place_kernel(core_ref, own_ref, other_ref, out_ref):
    first = core_ref[0] == 0
    own, other = own_ref[...], other_ref[...]
    for slot, value in ((0, jnp.where(first, own, other)), (1, jnp.where(first, other, own))):
        hi, lo = halves(value)
        out_ref[slot, 0] = hi
        out_ref[slot, 1] = lo


def place(core, own, other):
    n, depth = own.shape
    rows = 256
    block = pl.BlockSpec((rows, depth), lambda i, core: (i, 0))
    return pl.pallas_call(
        place_kernel,
        out_shape=jax.ShapeDtypeStruct((2, 2, n, depth), BF16),
        grid_spec=pltpu.PrefetchScalarGridSpec(
            num_scalar_prefetch=1,
            grid=(n // rows,),
            in_specs=[block, block],
            out_specs=pl.BlockSpec((2, 2, rows, depth), lambda i, core: (0, 0, i, 0)),
        ),
        compiler_params=params(),
        cost_estimate=cost(0, 16 * n * depth),
        name="place",
    )(core, own, other)


def weight(slot, first, rows, depth, steps):
    return pl.BlockSpec((None, 2, rows, depth), lambda i: (slot, 0, jnp.clip(i - first, 0, steps - 1), 0))


def whole(shape):
    return pl.BlockSpec(shape, lambda i: (0,) * len(shape))


def first_kernel(steps, rows, wi_ref, wl_ref, r_ref, s_ref, u_ref, cat_ref):
    i = pl.program_id(0)

    @pl.when(i == 0)
    def _():
        cat_ref[...] = joined(r_ref[...])

    @pl.when(i == steps)
    def _():
        cat_ref[...] = joined(s_ref[...])

    @pl.when(i < steps)
    def _():
        s_ref[pl.ds(pl.multiple_of(i * rows, rows), rows), :] = product(wi_ref, cat_ref[...])

    @pl.when(i >= steps)
    def _():
        u_ref[pl.ds(pl.multiple_of((i - steps) * rows, rows), rows), :] = product(wl_ref, cat_ref[...])


def first(wi, wl, r):
    n, width = r.shape
    rows = 256
    steps = n // rows
    out = jax.ShapeDtypeStruct((n, width), F32)
    return pl.pallas_call(
        functools.partial(first_kernel, steps, rows),
        out_shape=(out, out),
        grid=(2 * steps,),
        in_specs=[weight(0, 0, rows, n, steps), weight(0, steps, rows, n, steps), whole((n, width))],
        out_specs=(whole((n, width)), whole((n, width))),
        scratch_shapes=[pltpu.VMEM((n, 2 * width), BF16)],
        compiler_params=params(),
        cost_estimate=cost(12 * n * n * width, 8 * n * n),
        name="first",
    )(wi, wl, r)


def second_kernel(rows, wi_ref, r_ref, u_ref, s_ref, cat_ref):
    i = pl.program_id(0)

    @pl.when(i == 0)
    def _():
        cat_ref[...] = joined(r_ref[...] - u_ref[...])

    s_ref[...] = product(wi_ref, cat_ref[...])


def second(wi, r, u):
    n, width = r.shape
    rows = 256
    steps = n // rows
    return pl.pallas_call(
        functools.partial(second_kernel, rows),
        out_shape=jax.ShapeDtypeStruct((n, width), F32),
        grid=(steps,),
        in_specs=[weight(1, 0, rows, n, steps), whole((n, width)), whole((n, width))],
        out_specs=pl.BlockSpec((rows, width), lambda i: (i, 0)),
        scratch_shapes=[pltpu.VMEM((n, 2 * width), BF16)],
        compiler_params=params(),
        cost_estimate=cost(6 * n * n * width, 4 * n * n),
        name="second",
    )(wi, r, u)


def third_kernel(count, *refs):
    wl_ref, acc_ref, u_ref = refs[:3]
    parts, out_ref, cat_ref = refs[3 : 3 + count], refs[3 + count], refs[4 + count]

    @pl.when(pl.program_id(0) == 0)
    def _():
        cat_ref[...] = joined(sum(p[...] for p in parts))

    out_ref[...] = acc_ref[...] - u_ref[...] - product(wl_ref, cat_ref[...])


def third(wl, acc, u, parts):
    n, width = acc.shape
    rows = 256
    steps = n // rows
    tile = pl.BlockSpec((rows, width), lambda i: (i, 0))
    return pl.pallas_call(
        functools.partial(third_kernel, len(parts)),
        out_shape=jax.ShapeDtypeStruct((n, width), F32),
        grid=(steps,),
        in_specs=[weight(1, 0, rows, n, steps), tile, tile] + [whole((n, width))] * len(parts),
        out_specs=tile,
        scratch_shapes=[pltpu.VMEM((n, 2 * width), BF16)],
        compiler_params=params(),
        cost_estimate=cost(6 * n * n * width, 4 * n * n),
        name="third",
    )(wl, acc, u, *parts)


def update_kernel(keep_ref, w0_ref, w1_ref, s_ref, out_ref, cat_ref):
    @pl.when(pl.program_id(0) == 0)
    def _():
        for slot in range(2):
            cat_ref[slot] = joined(s_ref[slot])

    for a, w_ref in ((0, w0_ref), (1, w1_ref)):
        total = 0.0
        for slot in range(2):
            term = product(w_ref.at[slot], cat_ref[slot])
            total = total + (term * keep_ref[slot] if a == 0 else term)
        out_ref[0, a] = total


def update(keep, w0, w1, s):
    _, n, width = s.shape
    parts = 8
    rows = n // parts
    block = pl.BlockSpec((2, 2, rows, n), lambda i, keep: (0, 0, i, 0))
    return pl.pallas_call(
        update_kernel,
        out_shape=jax.ShapeDtypeStruct((parts, 2, rows, width), F32),
        grid_spec=pltpu.PrefetchScalarGridSpec(
            num_scalar_prefetch=1,
            grid=(parts,),
            in_specs=[block, block, pl.BlockSpec((2, n, width), lambda i, keep: (0, 0, 0))],
            out_specs=pl.BlockSpec((1, 2, rows, width), lambda i, keep: (i, 0, 0, 0)),
            scratch_shapes=[pltpu.VMEM((2, n, 2 * width), BF16)],
        ),
        compiler_params=params(),
        cost_estimate=cost(24 * n * n * width, 16 * n * n),
        name="update",
    )(keep, w0, w1, s)


def shards(panel, right_side, inverse_blocks):
    block = panel.shape[2]
    width = right_side.shape[3] // 2
    my_row, my_col = lax.axis_index("row"), lax.axis_index("col")
    row_count, col_count = lax.axis_size("row"), lax.axis_size("col")
    planes = row_count // 2
    plane, core = my_row // 2, my_row % 2
    core_arg = core.astype(jnp.int32).reshape(1)

    def send(array, moves):
        pairs = [
            ((2 * a + h) * col_count + b, (2 * c + h) * col_count + d)
            for (a, b), (c, d) in moves
            for h in range(2)
        ]
        return lax.ppermute(array, BOTH, pairs)

    def swap(array):
        return lax.ppermute(array, "row", [(r, r ^ 1) for r in range(row_count)])

    tiles = panel.reshape(2, block, block)
    inverse = inverse_blocks[0]
    my_half = lax.dynamic_slice_in_dim(right_side, core * width, width, 3).reshape(2, block, width)
    rhs = my_half[0]

    near = send(rhs, [((0, 0), (0, 1)), ((1, 0), (0, 2)), ((3, 0), (0, 3))])
    far = send(rhs, [((z, 0), (0, 4 + z)) for z in range(4)])
    wi = place(core_arg, inverse, swap(inverse))
    wl = place(core_arg, tiles[0], swap(tiles[0]))
    wl1 = place(core_arg, tiles[1], swap(tiles[1]))

    acc = jnp.where(plane == 0, rhs, jnp.zeros_like(rhs))
    r_p, r_q = near + far, acc
    kept = []
    for m in range(planes):
        low, high = 2 * m, 2 * m + 1
        nxt, last = 2 * m + 2, 2 * m + 3
        s_p, u = first(wi, wl, r_p)
        s_q = second(wi, r_q, u)
        kept.append((s_p, s_q))
        if m == planes - 1:
            break
        to_next = send(s_q, [((m, high), (m, nxt))])
        to_last = send(s_q, [((m, high), (m, last))])
        soon = third(wl, acc, u, [to_next, to_last])
        q_part = send(soon, [((m, nxt), (m + 1, last))])
        other = [((m, last), (m + 1, last))]
        if m < planes - 2:
            other += [((m, nxt), (m + 1, nxt + 2))]
        mixed = send(soon, other)
        is_high = my_col == last
        r_p = q_part
        r_q = mixed
        if m < planes - 2:
            r_p = r_p + jnp.where(is_high, 0.0, mixed)
            r_p = r_p + send(soon, [((m, nxt), (m + 1, nxt + 3))])
            has = jnp.where(my_col == high, s_q, to_next + to_last)
            if m == 0:
                late = [send(has, [((0, 1), (0, 5)), ((0, 2), (0, 6)), ((0, 3), (0, 7))]), send(has, [((0, 1), (0, 4))])]
                r_p = r_p + send(soon, [((0, 2), (1, 6))]) + send(soon, [((0, 2), (1, 7))])
            else:
                late = [send(has, [((1, 3), (1, 7)), ((1, 5), (1, 6))])]
            later = third(wl, acc, u, late)
            moved = send(later, [((m, c), (m + 1, c)) for c in range(nxt + 2, 8)])
            acc = jnp.where(plane == m + 1, moved, acc)

    mine = jnp.stack([sum(s for s, _ in kept), sum(s for _, s in kept)])
    cut = 2 * block // col_count
    pieces = lax.all_to_all(mine.reshape(col_count, cut, width), "col", 0, 0)
    piece = lax.dynamic_index_in_dim(pieces, 2 * plane + 1, 0, keepdims=True)
    pieces = lax.all_to_all(jnp.broadcast_to(piece, pieces.shape), "col", 0, 0)
    mine = pieces.reshape(2, block, width)

    keep = (my_col > 2 * plane + jnp.arange(2)).astype(F32)
    parts = update(keep, wl, wl1, mine)
    parts = lax.all_to_all(parts, "row", 0, 0)
    share = block // row_count
    sums = parts.reshape(planes, 2, 2, share, width).sum(0)
    sums = jnp.concatenate([sums[0], sums[1]], axis=-1)
    own = lax.dynamic_slice_in_dim(right_side, my_row * share, share, 2).reshape(2, share, 2 * width)
    updated = (own - sums).reshape(2, 1, share, 2 * width)

    ours = jnp.where(core == 0, mine[0], mine[1])
    theirs = swap(jnp.where(core == 0, mine[1], mine[0]))
    solved = jnp.concatenate([jnp.where(core == 0, ours, theirs), jnp.where(core == 0, theirs, ours)], axis=1)
    return solved.reshape(1, block, 2 * width), updated


def solution(mesh):
    placed = (P(None, "col", None, "row", None), P(None, "col", None, None), P("row", None, None))
    return jax.shard_map(
        shards,
        mesh=mesh,
        in_specs=placed,
        out_specs=(P("row", None, None), P(None, "col", "row", None)),
        check_vma=False,
    )
```

```python
import functools

import jax
import jax.numpy as jnp
from jax import lax
from jax.experimental import pallas as pl
from jax.experimental.pallas import tpu as pltpu
from jax.sharding import PartitionSpec as P

F32 = jnp.float32
BF16 = jnp.bfloat16
LIMIT = 32 * 1024 * 1024
SMALL = 16 * 1024 * 1024
BOTH = ("row", "col")


def halves(x):
    hi = x.astype(BF16)
    return hi, (x - hi.astype(F32)).astype(BF16)


def joined(x):
    return jnp.concatenate(halves(x), axis=1)


def product(w, cat):
    width = cat.shape[1] // 2
    one = jnp.dot(w[0], cat, preferred_element_type=F32)
    two = jnp.dot(w[1], cat[:, :width], preferred_element_type=F32)
    return one[:, :width] + one[:, width:] + two


def cost(flops, nbytes):
    return pl.CostEstimate(flops=flops, bytes_accessed=nbytes, transcendentals=0)


def params():
    return pltpu.CompilerParams(vmem_limit_bytes=LIMIT)


def place_kernel(core_ref, own_ref, other_ref, out_ref):
    core = core_ref[0]
    for slot, ref in ((core, own_ref), (1 - core, other_ref)):
        hi, lo = halves(ref[...])
        out_ref[slot, 0] = hi
        out_ref[slot, 1] = lo


def place(core, own, other):
    n, depth = own.shape
    rows = 256
    block = pl.BlockSpec((rows, depth), lambda i, core: (i, 0))
    return pl.pallas_call(
        place_kernel,
        out_shape=jax.ShapeDtypeStruct((2, 2, n, depth), BF16),
        grid_spec=pltpu.PrefetchScalarGridSpec(
            num_scalar_prefetch=1,
            grid=(n // rows,),
            in_specs=[block, block],
            out_specs=pl.BlockSpec((2, 2, rows, depth), lambda i, core: (0, 0, i, 0)),
        ),
        compiler_params=params(),
        cost_estimate=cost(0, 16 * n * depth),
        name="place",
    )(core, own, other)


def vmem(count):
    return [pl.BlockSpec(memory_space=pltpu.VMEM)] * count


def call(kernel, name, products, outs, *args):
    n, width = outs[0]
    return pl.pallas_call(
        kernel,
        out_shape=tuple(jax.ShapeDtypeStruct(shape, F32) for shape in outs),
        in_specs=vmem(len(args)),
        out_specs=tuple(vmem(len(outs))),
        compiler_params=pltpu.CompilerParams(vmem_limit_bytes=SMALL),
        cost_estimate=cost(6 * products * n * n * width, 4 * products * n * n),
        name=name,
    )(*args)


def first_kernel(wi_ref, wl_ref, r_ref, s_ref, u_ref):
    s = product(wi_ref.at[0], joined(r_ref[...]))
    s_ref[...] = s
    u_ref[...] = product(wl_ref.at[0], joined(s))


def first(wi, wl, r):
    return call(first_kernel, "first", 2, [r.shape] * 2, wi, wl, r)


def second_kernel(wi_ref, r_ref, u_ref, s_ref):
    s_ref[...] = product(wi_ref.at[1], joined(r_ref[...] - u_ref[...]))


def second(wi, r, u):
    return call(second_kernel, "second", 1, [r.shape], wi, r, u)[0]


def third_kernel(wl_ref, acc_ref, u_ref, *refs):
    parts, out_ref = refs[:-1], refs[-1]
    s = functools.reduce(jnp.add, [p[...] for p in parts])
    out_ref[...] = acc_ref[...] - u_ref[...] - product(wl_ref.at[1], joined(s))


def third(wl, acc, u, parts):
    return call(third_kernel, "third", 1, [acc.shape], wl, acc, u, *parts)[0]


def pair_kernel(wi_ref, wl_ref, wq_ref, even_ref, a_ref, b_ref, acc_ref, p_ref, q_ref, out_ref):
    even = even_ref[0] == 1
    a, b = a_ref[...], b_ref[...]
    s_p = product(wi_ref.at[0], joined(jnp.where(even, a, b)))
    p_ref[...] = s_p
    cat = joined(s_p)
    rest = jnp.where(even, b, a) - product(wq_ref, cat)
    s_q = product(wi_ref.at[1], joined(rest))
    q_ref[...] = s_q
    out_ref[...] = acc_ref[...] - product(wl_ref.at[0], cat) - product(wl_ref.at[1], joined(s_q))


def pair(wi, wl, wq, even, a, b, acc):
    specs = vmem(3) + [pl.BlockSpec(memory_space=pltpu.SMEM)] + vmem(3)
    n, width = a.shape
    out = jax.ShapeDtypeStruct((n, width), F32)
    return pl.pallas_call(
        pair_kernel,
        out_shape=(out, out, out),
        in_specs=specs,
        out_specs=tuple(vmem(3)),
        compiler_params=pltpu.CompilerParams(vmem_limit_bytes=SMALL),
        cost_estimate=cost(30 * n * n * width, 20 * n * n),
        name="pair",
    )(wi, wl, wq, even, a, b, acc)


def less_kernel(wl_ref, p_ref, q_ref, acc_ref, out_ref):
    out_ref[...] = (
        acc_ref[...] - product(wl_ref.at[0], joined(p_ref[...])) - product(wl_ref.at[1], joined(q_ref[...]))
    )


def less(wl, p, q, acc):
    return call(less_kernel, "less", 2, [acc.shape], wl, p, q, acc)[0]


def join_kernel(core_ref, own_ref, other_ref, out_ref):
    core = core_ref[0]
    n = own_ref.shape[0]
    for half, ref in ((core, own_ref), (1 - core, other_ref)):
        hi, lo = halves(ref[...])
        rows = pl.ds(pl.multiple_of(half * n, n), n)
        out_ref[0, rows, :] = hi
        out_ref[1, rows, :] = lo


def join(core, own, other):
    n, depth = own.shape
    return pl.pallas_call(
        join_kernel,
        out_shape=jax.ShapeDtypeStruct((2, 2 * n, depth), BF16),
        in_specs=[pl.BlockSpec(memory_space=pltpu.SMEM)] + vmem(2),
        out_specs=vmem(1)[0],
        compiler_params=pltpu.CompilerParams(vmem_limit_bytes=SMALL),
        cost_estimate=cost(0, 16 * n * depth),
        name="join",
    )(core, own, other)


def update_kernel(keep_ref, w0_ref, w1_ref, s_ref, out_ref, cat_ref):
    @pl.when(pl.program_id(0) == 0)
    def _():
        for slot in range(2):
            cat_ref[slot] = joined(s_ref[slot])

    for a, w_ref in ((0, w0_ref), (1, w1_ref)):
        total = 0.0
        for slot in range(2):
            term = product(w_ref.at[slot], cat_ref[slot])
            total = total + (term * keep_ref[slot] if a == 0 else term)
        out_ref[0, a] = total


def update(keep, w0, w1, s):
    _, n, width = s.shape
    parts = 8
    rows = n // parts
    block = pl.BlockSpec((2, 2, rows, n), lambda i, keep: (0, 0, i, 0))
    return pl.pallas_call(
        update_kernel,
        out_shape=jax.ShapeDtypeStruct((parts, 2, rows, width), F32),
        grid_spec=pltpu.PrefetchScalarGridSpec(
            num_scalar_prefetch=1,
            grid=(parts,),
            in_specs=[block, block, pl.BlockSpec((2, n, width), lambda i, keep: (0, 0, 0))],
            out_specs=pl.BlockSpec((1, 2, rows, width), lambda i, keep: (i, 0, 0, 0)),
            scratch_shapes=[pltpu.VMEM((2, n, 2 * width), BF16)],
        ),
        compiler_params=params(),
        cost_estimate=cost(24 * n * n * width, 16 * n * n),
        name="update",
    )(keep, w0, w1, s)


def shards(panel, right_side, inverse_blocks):
    block = panel.shape[2]
    width = right_side.shape[3] // 2
    my_row, my_col = lax.axis_index("row"), lax.axis_index("col")
    row_count, col_count = lax.axis_size("row"), lax.axis_size("col")
    planes = row_count // 2
    plane, core = my_row // 2, my_row % 2
    core_arg = core.astype(jnp.int32).reshape(1)

    def send(array, moves):
        pairs = [
            ((2 * a + h) * col_count + b, (2 * c + h) * col_count + d)
            for (a, b), (c, d) in moves
            for h in range(2)
        ]
        return lax.ppermute(array, BOTH, pairs)

    def swap(array):
        return lax.ppermute(array, "row", [(r, r ^ 1) for r in range(row_count)])

    inverse = inverse_blocks[0]
    my_half = lax.dynamic_slice_in_dim(right_side, core * width, width, 3).reshape(2, block, width)
    rhs = my_half[0]
    even = (1 - my_col % 2).astype(jnp.int32).reshape(1)

    near = send(rhs, [((0, 0), (0, 1)), ((1, 0), (0, 2)), ((3, 0), (0, 3))])
    far = send(rhs, [((z, 0), (0, 4 + z)) for z in range(4)])
    other_inverse = swap(inverse)
    tile = panel[0, 0, :, 0, :]
    other_tile = swap(tile)
    wi = place(core_arg, inverse, other_inverse)
    wl = place(core_arg, tile, other_tile)

    half = block // 2
    coupling = jnp.where(core == 0, tile[:half], other_tile[half:])
    got = send(coupling, [((1, 3), (1, 4)), ((2, 5), (2, 6))])
    quarter = half // 2
    via = [send(coupling[i * quarter : (i + 1) * quarter], [((2, 5), (2, 7)), ((1, 3), (1, 1))]) for i in range(2)]
    on = [send(v, [((1, 1), (1, 5))]) for v in via]
    got = got + jnp.concatenate([jnp.where(plane == 2, v, o) for v, o in zip(via, on)])
    wq = join(core_arg, got, swap(got))

    acc = jnp.where(plane == 0, rhs, jnp.zeros_like(rhs))
    s_p, u = first(wi, wl, near + far)
    s_q = second(wi, acc, u)
    kept = [(s_p, s_q)]
    to_2 = send(s_q, [((0, 1), (0, 2))])
    to_3 = send(s_q, [((0, 1), (0, 3))])
    soon = third(wl, acc, u, [to_2, to_3])
    a = send(soon, [((0, 2), (1, 4)), ((0, 3), (1, 5))])
    b = send(soon, [((0, 2), (1, 5)), ((0, 3), (1, 4))])
    has = jnp.where(my_col == 1, s_q, to_2 + to_3)
    late = [send(has, [((0, 1), (0, 5)), ((0, 2), (0, 6)), ((0, 3), (0, 7))]), send(has, [((0, 1), (0, 4))])]
    later = third(wl, acc, u, late)
    acc = send(later, [((0, c), (1, c)) for c in range(4, 8)])

    s_p, s_q, soon = pair(wi, wl, wq, even, a, b, acc)
    kept.append((s_p, s_q))
    a = send(soon, [((1, 4), (2, 6)), ((1, 5), (2, 7))])
    b = send(soon, [((1, 4), (2, 7)), ((1, 5), (2, 6))])
    late = [send(s, [((1, 4), (1, 6)), ((1, 5), (1, 7))]) for s in (s_p, s_q)]
    later = less(wl, *late, acc)
    acc = send(later, [((1, c), (2, c)) for c in (6, 7)])

    s_p, s_q, soon = pair(wi, wl, wq, even, a, b, acc)
    kept.append((s_p, s_q))
    r_p = send(soon, [((2, 6), (3, 7))])
    r_q = send(soon, [((2, 7), (3, 7))])

    s_p, u = first(wi, wl, r_p)
    s_q = second(wi, r_q, u)
    kept.append((s_p, s_q))
    other_panel = swap(panel[1, 0, :, 0, :])
    wl1 = place(core_arg, panel[1, 0, :, 0, :], other_panel)

    mine = jnp.stack([sum(s for s, _ in kept), sum(s for _, s in kept)])
    cut = 2 * block // col_count
    pieces = lax.all_to_all(mine.reshape(col_count, cut, width), "col", 0, 0)
    root = jnp.array([1, 4, 6, 7])[plane]
    piece = lax.dynamic_index_in_dim(pieces, root, 0, keepdims=True)
    pieces = lax.all_to_all(jnp.broadcast_to(piece, pieces.shape), "col", 0, 0)
    mine = pieces.reshape(2, block, width)

    keep = (my_col > 2 * plane + jnp.arange(2)).astype(F32)
    parts = update(keep, wl, wl1, mine)
    parts = lax.all_to_all(parts, "row", 0, 0)
    share = block // row_count
    sums = parts.reshape(planes, 2, 2, share, width).sum(0)
    sums = jnp.concatenate([sums[0], sums[1]], axis=-1)
    own = lax.dynamic_slice_in_dim(right_side, my_row * share, share, 2).reshape(2, share, 2 * width)
    updated = (own - sums).reshape(2, 1, share, 2 * width)

    ours = jnp.where(core == 0, mine[0], mine[1])
    theirs = swap(jnp.where(core == 0, mine[1], mine[0]))
    solved = jnp.concatenate([jnp.where(core == 0, ours, theirs), jnp.where(core == 0, theirs, ours)], axis=1)
    return solved.reshape(1, block, 2 * width), updated


def solution(mesh):
    placed = (P(None, "col", None, "row", None), P(None, "col", None, None), P("row", None, None))
    return jax.shard_map(
        shards,
        mesh=mesh,
        in_specs=placed,
        out_specs=(P("row", None, None), P(None, "col", "row", None)),
        check_vma=False,
    )
```

```python
import functools

import jax
import jax.numpy as jnp
from jax import lax
from jax.experimental import pallas as pl
from jax.experimental.pallas import tpu as pltpu
from jax.sharding import PartitionSpec as P

F32 = jnp.float32
BF16 = jnp.bfloat16
LIMIT = 16 * 1024 * 1024
BOTH = ("row", "col")
VMEM = pl.BlockSpec(memory_space=pltpu.VMEM)
SMEM = pl.BlockSpec(memory_space=pltpu.SMEM)
ANY = pl.BlockSpec(memory_space=pl.ANY)


def halves(x):
    hi = x.astype(BF16)
    return hi, (x - hi.astype(F32)).astype(BF16)


def joined(x):
    return jnp.concatenate(halves(x), axis=1)


def product(w, cat):
    width = cat.shape[1] // 2
    one = jnp.dot(w[0], cat, preferred_element_type=F32)
    two = jnp.dot(w[1], cat[:, :width], preferred_element_type=F32)
    return one[:, :width] + one[:, width:] + two


def packed(x, half):
    n, width = x.shape
    part = x[:, half * width // 2 : (half + 1) * width // 2]
    return jnp.concatenate([part[: n // 2], part[n // 2 :]], axis=1)


def unpacked(x):
    width = x.shape[1] // 2
    return jnp.concatenate([x[:, :width], x[:, width:]], axis=0)


def cost(flops, nbytes):
    return pl.CostEstimate(flops=1, bytes_accessed=1, transcendentals=0)


def call(kernel, name, products, outs, specs, *args):
    n = 1024
    return pl.pallas_call(
        kernel,
        out_shape=tuple(jax.ShapeDtypeStruct(shape, kind) for shape, kind in outs),
        in_specs=specs,
        out_specs=(VMEM,) * len(outs),
        compiler_params=pltpu.CompilerParams(vmem_limit_bytes=LIMIT),
        cost_estimate=cost(6 * products * n * n * 128, 4 * products * n * n),
        name=name,
    )(*args)


def after(x, *others):
    return lax.optimization_barrier((x,) + others)[0]


def retile_kernel(a, panel_ref, out_ref, sem):
    copy = pltpu.make_async_copy(panel_ref.at[a, 0, :, 0], out_ref, sem.at[0])
    copy.start()
    copy.wait()


def retile(panel, a):
    n, depth = panel.shape[2], panel.shape[4]
    return pl.pallas_call(
        functools.partial(retile_kernel, a),
        out_shape=jax.ShapeDtypeStruct((n, depth), F32),
        in_specs=[pl.BlockSpec(memory_space=pltpu.HBM)],
        out_specs=VMEM,
        scratch_shapes=[pltpu.SemaphoreType.DMA((1,))],
        compiler_params=pltpu.CompilerParams(vmem_limit_bytes=(56 - 40 * a) * 1024 * 1024),
        cost_estimate=cost(0, 8 * n * depth),
        name="retile",
    )(panel)


def place_kernel(core_ref, own_ref, other_ref, out_ref, *ahead):
    core = core_ref[0]
    for slot, ref in ((core, own_ref), (1 - core, other_ref)):
        hi, lo = halves(ref[...])
        out_ref[slot, 0] = hi
        out_ref[slot, 1] = lo
    step = pl.program_id(0)
    rows = own_ref.shape[0]
    for ahead_ref in ahead:
        for h, ref in ((0, own_ref), (1, other_ref)):

            @pl.when((core == h) & (step // 2 == h))
            def _():
                ahead_ref[pl.ds(pl.multiple_of((step - 2 * h) * rows, rows), rows), :] = ref[...]


def place(core, own, other, ahead):
    n, depth = own.shape
    rows = n // 4
    block = pl.BlockSpec((rows, depth), lambda i, core: (i, 0))
    still = pl.BlockSpec((n // 2, depth), lambda i, core: (0, 0))
    return pl.pallas_call(
        place_kernel,
        out_shape=[jax.ShapeDtypeStruct((2, 2, n, depth), BF16)] + [jax.ShapeDtypeStruct((n // 2, depth), F32)] * ahead,
        grid_spec=pltpu.PrefetchScalarGridSpec(
            num_scalar_prefetch=1,
            grid=(4,),
            in_specs=[block, block],
            out_specs=[pl.BlockSpec((2, 2, rows, depth), lambda i, core: (0, 0, i, 0))] + [still] * ahead,
        ),
        compiler_params=pltpu.CompilerParams(vmem_limit_bytes=LIMIT),
        cost_estimate=cost(0, 16 * n * depth),
        name="place",
    )(core, own, other)


def first_kernel(wi_ref, wl_ref, flag_ref, a_ref, b_ref, c_ref, s_ref, u_ref):
    r = a_ref[...] + c_ref[...] + b_ref[...] * flag_ref[0].astype(F32)
    s = product(wi_ref.at[0], joined(r))
    s_ref[...] = s
    u_ref[...] = product(wl_ref.at[0], joined(s))


def second_kernel(wi_ref, r_ref, u_ref, s_ref):
    s_ref[...] = product(wi_ref.at[1], joined(r_ref[...] - u_ref[...]))


def third_kernel(wl_ref, acc_ref, u_ref, *refs):
    parts, out_ref, sum_ref = refs[:-2], refs[-2], refs[-1]
    s = functools.reduce(jnp.add, [p[...] for p in parts])
    sum_ref[...] = s
    out_ref[...] = acc_ref[...] - u_ref[...] - product(wl_ref.at[1], joined(s))


def both_ways(even, x, one_ref, two_ref):
    low, high = packed(x, 0), packed(x, 1)
    one_ref[...] = jnp.where(even, low, high)
    two_ref[...] = jnp.where(even, high, low)


def pair_kernel(wi_ref, wl_ref, wq_ref, even_ref, a_ref, b_ref, one_ref, two_ref, p_ref, q_ref):
    even = even_ref[0] == 1
    a, b = a_ref[...], b_ref[...]
    s_p = product(wi_ref.at[0], joined(jnp.where(even, a, b)))
    cat = joined(s_p)
    rest = jnp.where(even, b, a) - product(wq_ref, cat)
    s_q = product(wi_ref.at[1], joined(rest))
    part = product(wl_ref.at[0], cat) + product(wl_ref.at[1], joined(s_q))
    both_ways(even, -part, one_ref, two_ref)
    p_ref[...] = s_p
    q_ref[...] = s_q


def less_kernel(wl_ref, even_ref, p_ref, q_ref, acc_ref, one_ref, two_ref):
    part = product(wl_ref.at[0], joined(p_ref[...])) + product(wl_ref.at[1], joined(q_ref[...]))
    both_ways(even_ref[0] == 1, acc_ref[...] - part, one_ref, two_ref)


def merge_kernel(own_ref, x_ref, y_ref, mine_ref, out_ref):
    out_ref[...] = x_ref[...] + y_ref[...] + mine_ref[...] * own_ref[0].astype(F32)


def join_kernel(core_ref, own_ref, other_ref, out_ref):
    core = core_ref[0]
    n = own_ref.shape[0]
    for half, ref in ((core, own_ref), (1 - core, other_ref)):
        hi, lo = halves(ref[...])
        rows = pl.ds(pl.multiple_of(half * n, n), n)
        out_ref[0, rows, :] = hi
        out_ref[1, rows, :] = lo


def final_kernel(wi_ref, wq_ref, even_ref, a_ref, b_ref, c_ref, d_ref, *refs):
    known, out_ref = refs[:-1], refs[-1]
    even = even_ref[0] == 1
    one, two = a_ref[...] + c_ref[...], b_ref[...] + d_ref[...]
    s_p = product(wi_ref.at[0], joined(unpacked(jnp.where(even, one, two))))
    rest = unpacked(jnp.where(even, two, one)) - product(wq_ref, joined(s_p))
    s_q = product(wi_ref.at[1], joined(rest))
    n = s_p.shape[0] // 2
    for slot, s in ((0, s_p), (1, s_q)):
        old = functools.reduce(jnp.add, [k[...] for k in known[slot::2]])
        old = jnp.where(even, packed(old, 0), packed(old, 1))
        out_ref[slot] = old + jnp.concatenate([s[:n], s[n:]], axis=1)


def update_kernel(keep_ref, w0_ref, w1_ref, s_ref, out_ref, solved_ref):
    parts, _, rows, width = out_ref.shape
    steps, cuts = s_ref.shape[0] // 2, s_ref.shape[1]
    for slot in range(2):
        sides = []
        for half in range(cuts):
            pieces = [s_ref[slot * steps + j, half] for j in range(steps)]
            sides.append(unpacked(jnp.concatenate(pieces, axis=0)))
        solved_ref[slot] = jnp.concatenate(sides, axis=1)
    cats = [joined(solved_ref[slot]) for slot in range(2)]
    for a, w_ref in ((0, w0_ref), (1, w1_ref)):
        terms = [product(w_ref.at[slot], cats[slot]) for slot in range(2)]
        if a == 0:
            terms = [t * keep_ref[slot] for slot, t in enumerate(terms)]
        total = terms[0] + terms[1]
        for j in range(parts):
            out_ref[j, a] = total[j * rows : (j + 1) * rows]


def shards(panel, right_side, inverse_blocks):
    block = panel.shape[2]
    width = right_side.shape[3] // 2
    my_row, my_col = lax.axis_index("row"), lax.axis_index("col")
    row_count, col_count = lax.axis_size("row"), lax.axis_size("col")
    planes = row_count // 2
    plane, core = my_row // 2, my_row % 2
    core_arg = core.astype(jnp.int32).reshape(1)
    even = (1 - my_col % 2).astype(jnp.int32).reshape(1)
    whole = ((block, width), F32)
    slim = ((block // 2, width), F32)

    def send(array, moves):
        pairs = [
            ((2 * a + h) * col_count + b, (2 * c + h) * col_count + d)
            for (a, b), (c, d) in moves
            for h in range(2)
        ]
        return lax.ppermute(array, BOTH, pairs)

    def swap(array):
        return lax.ppermute(array, "row", [(r, r ^ 1) for r in range(row_count)])

    def flag(condition):
        return condition.astype(jnp.int32).reshape(1)

    inverse = inverse_blocks[0]
    rhs = lax.dynamic_slice(right_side, (0, 0, 0, core * width), (1, 1, block, width)).reshape(block, width)
    near = send(rhs, [((0, 0), (0, 1)), ((1, 0), (0, 2)), ((3, 0), (0, 3))])
    other_inverse = swap(inverse)
    tile = retile(after(panel, rhs), 0)
    other_tile = swap(tile)
    far = send(after(rhs, tile), [((z, 0), (0, 4 + z)) for z in range(4)])
    (wi,) = place(core_arg, inverse, other_inverse, 0)
    wl, ahead = place(core_arg, tile, after(other_tile, near), 1)

    firsts, thirds = [VMEM] * 2 + [SMEM] + [VMEM] * 3, [VMEM] * 5
    one = jnp.zeros((1,), jnp.int32)
    p_0, u = call(first_kernel, "first", 2, [whole] * 2, firsts, wi, wl, one, near, far, far)
    (s_q,) = call(second_kernel, "second", 1, [whole], [VMEM] * 3, wi, rhs, u)
    to_2 = send(s_q, [((0, 1), (0, 2))])
    to_3 = send(s_q, [((0, 1), (0, 3))])

    tile = retile(after(panel, s_q), 1)
    (wl1,) = place(core_arg, tile, swap(tile), 0)
    x = send(after(ahead, s_q), [((2, 5), (2, 6)), ((3, 7), (3, 6))])
    y = send(after(ahead, s_q), [((2, 5), (2, 7))])

    soon, q_0 = call(third_kernel, "third", 1, [whole] * 2, thirds, wl, rhs, u, after(to_2, wl1), to_3)
    a = send(soon, [((0, 2), (1, 3))])
    b = send(soon, [((0, 3), (1, 3)), ((0, 2), (1, 4))])
    c = send(soon, [((0, 2), (1, 5))])
    late_5 = send(after(s_q, soon), [((0, 1), (0, 5))])
    late_4 = send(after(s_q, soon), [((0, 1), (0, 4))])
    late_6 = send(q_0, [((0, 2), (0, 6)), ((0, 3), (0, 7))])
    later, _ = call(third_kernel, "later", 1, [whole] * 2, thirds + [VMEM], wl, rhs, u, late_4, late_5, late_6)
    acc = send(later, [((0, c), (1, c)) for c in range(4, 8)])

    own_flag = flag((plane == 3) & (my_col == 7))
    (got,) = call(
        merge_kernel, "merge", 0, [((block // 2, block), F32)], [SMEM] + [VMEM] * 3, own_flag, after(x, soon), y, ahead
    )
    wq = call(join_kernel, "join", 0, [((2, block, block), BF16)], [SMEM] + [VMEM] * 2, core_arg, got, swap(got))[0]

    a = after(a, wq)
    not_3 = flag(my_col != 3)
    p_1, u = call(first_kernel, "first", 2, [whole] * 2, firsts, wi, wl, not_3, a, b, c)
    (s_q,) = call(second_kernel, "second", 1, [whole], [VMEM] * 3, wi, b, u)
    to_4 = send(s_q, [((1, 3), (1, 4))])
    to_5 = send(s_q, [((1, 3), (1, 5))])

    soon, q_1 = call(third_kernel, "third", 1, [whole] * 2, thirds, wl, acc, u, to_4, to_5)
    a = send(soon, [((1, 4), (2, 6)), ((1, 5), (2, 7))])
    b = send(soon, [((1, 4), (2, 7)), ((1, 5), (2, 6))])
    late = [send(s, [((1, 4), (1, 6)), ((1, 5), (1, 7))]) for s in (p_1, q_1)]
    one, two = call(less_kernel, "less", 2, [slim] * 2, [VMEM, SMEM] + [VMEM] * 3, wl, even, *late, acc)
    c = send(one, [((1, 6), (3, 6)), ((1, 7), (3, 7))])
    d = send(two, [((1, 6), (3, 7)), ((1, 7), (3, 6))])

    specs = [VMEM] * 3 + [SMEM] + [VMEM] * 2
    one, two, p_2, q_2 = call(pair_kernel, "pair", 5, [slim] * 2 + [whole] * 2, specs, wi, wl, wq, even, a, b)
    a = send(one, [((2, 6), (3, 6)), ((2, 7), (3, 7))])
    b = send(two, [((2, 6), (3, 7)), ((2, 7), (3, 6))])

    specs = [VMEM] * 2 + [SMEM] + [VMEM] * 10
    known = (p_0, q_0, p_1, q_1, p_2, q_2)
    (mine,) = call(
        final_kernel, "final", 3, [((2, block // 2, width), F32)], specs, wi, wq, even, a, b, c, d, *known
    )

    cut = block // col_count
    pieces = lax.all_to_all(mine.reshape(col_count, cut, width), "col", 0, 0)
    root = jnp.array([2, 4, 6, 6])[plane]
    piece = lax.dynamic_slice_in_dim(pieces, root, 2, 0)
    pieces = lax.all_to_all(jnp.broadcast_to(piece[None], (col_count, 2, cut, width)), "col", 0, 0)

    keep = (my_col > 2 * plane + jnp.arange(2)).astype(F32)
    share = block // row_count
    outs = [((row_count, 2, share, width), F32), ((2, block, width), F32)]
    parts, mine = call(update_kernel, "update", 4, outs, [SMEM] + [VMEM] * 3, keep, wl, wl1, pieces)
    parts = lax.all_to_all(parts, "row", 0, 0)
    sums = parts.reshape(planes, 2, 2, share, width).sum(0)
    sums = jnp.concatenate([sums[0], sums[1]], axis=-1)
    own = lax.dynamic_slice_in_dim(right_side, my_row * share, share, 2).reshape(2, share, 2 * width)
    updated = (own - sums).reshape(2, 1, share, 2 * width)

    ours = jnp.where(core == 0, mine[0], mine[1])
    theirs = swap(jnp.where(core == 0, mine[1], mine[0]))
    solved = jnp.concatenate([jnp.where(core == 0, ours, theirs), jnp.where(core == 0, theirs, ours)], axis=1)
    return solved.reshape(1, block, 2 * width), updated


def solution(mesh):
    placed = (P(None, "col", None, "row", None), P(None, "col", None, None), P("row", None, None))
    return jax.shard_map(
        shards,
        mesh=mesh,
        in_specs=placed,
        out_specs=(P("row", None, None), P(None, "col", "row", None)),
        check_vma=False,
    )
```

```python
import functools

import jax
import jax.numpy as jnp
from jax import lax
from jax.experimental import pallas as pl
from jax.experimental.pallas import tpu as pltpu
from jax.sharding import PartitionSpec as P

F32 = jnp.float32
BF16 = jnp.bfloat16
LIMIT = 12 * 1024 * 1024
BOTH = ("row", "col")
VMEM = pl.BlockSpec(memory_space=pltpu.VMEM)
SMEM = pl.BlockSpec(memory_space=pltpu.SMEM)
ANY = pl.BlockSpec(memory_space=pl.ANY)


def halves(x):
    hi = x.astype(BF16)
    return hi, (x - hi.astype(F32)).astype(BF16)


def joined(x):
    return jnp.concatenate(halves(x), axis=1)


def product(w, cat):
    width = cat.shape[1] // 2
    hi, lo = halves(w)
    one = jnp.dot(hi, cat, preferred_element_type=F32)
    two = jnp.dot(lo, cat[:, :width], preferred_element_type=F32)
    return one[:, :width] + one[:, width:] + two


class Pair:
    def __init__(self, core_ref, own_ref, other_ref):
        self.first, self.refs = core_ref[0] == 0, (own_ref, other_ref)

    def __getitem__(self, slot):
        own, other = (ref[...] for ref in self.refs)
        return jnp.where(self.first, own, other) if slot == 0 else jnp.where(self.first, other, own)


def stacked(core_ref, own_ref, other_ref, cat):
    first = core_ref[0] == 0
    own, other = product(own_ref[...], cat), product(other_ref[...], cat)
    return jnp.concatenate([jnp.where(first, own, other), jnp.where(first, other, own)], axis=0)


def packed(x, half):
    n, width = x.shape
    part = x[:, half * width // 2 : (half + 1) * width // 2]
    return jnp.concatenate([part[: n // 2], part[n // 2 :]], axis=1)


def unpacked(x):
    width = x.shape[1] // 2
    return jnp.concatenate([x[:, :width], x[:, width:]], axis=0)


def cost(flops, nbytes):
    return pl.CostEstimate(flops=flops, bytes_accessed=nbytes, transcendentals=0)


def call(kernel, name, products, outs, specs, *args):
    n = 1024
    return pl.pallas_call(
        kernel,
        out_shape=tuple(jax.ShapeDtypeStruct(shape, kind) for shape, kind in outs),
        in_specs=specs,
        out_specs=(VMEM,) * len(outs),
        compiler_params=pltpu.CompilerParams(vmem_limit_bytes=LIMIT),
        cost_estimate=cost(6 * products * n * n * 128, 4 * products * n * n),
        name=name,
    )(*args)


def after(x, *others):
    return lax.optimization_barrier((x,) + others)[0]


def retile_kernel(a, panel_ref, out_ref, sem):
    copy = pltpu.make_async_copy(panel_ref.at[a, 0, :, 0], out_ref, sem.at[0])
    copy.start()
    copy.wait()


def retile(panel, a):
    n, depth = panel.shape[2], panel.shape[4]
    return pl.pallas_call(
        functools.partial(retile_kernel, a),
        out_shape=jax.ShapeDtypeStruct((n, depth), F32),
        in_specs=[pl.BlockSpec(memory_space=pltpu.HBM)],
        out_specs=VMEM,
        scratch_shapes=[pltpu.SemaphoreType.DMA((1,))],
        compiler_params=pltpu.CompilerParams(vmem_limit_bytes=(56 - 40 * a) * 1024 * 1024),
        cost_estimate=cost(0, 8 * n * depth),
        name="retile",
    )(panel)


def cut_kernel(core_ref, own_ref, other_ref, out_ref):
    n = out_ref.shape[0]

    @pl.when(core_ref[0] == 0)
    def _():
        out_ref[...] = own_ref[:n]

    @pl.when(core_ref[0] == 1)
    def _():
        out_ref[...] = other_ref[n:]


def first_kernel(core_ref, flag_ref, io_ref, ix_ref, lo_ref, lx_ref, a_ref, b_ref, c_ref, s_ref, u_ref):
    r = a_ref[...] + c_ref[...] + b_ref[...] * flag_ref[0].astype(F32)
    s = product(Pair(core_ref, io_ref, ix_ref)[0], joined(r))
    s_ref[...] = s
    u_ref[...] = product(Pair(core_ref, lo_ref, lx_ref)[0], joined(s))


def second_kernel(core_ref, io_ref, ix_ref, r_ref, u_ref, s_ref):
    s_ref[...] = product(Pair(core_ref, io_ref, ix_ref)[1], joined(r_ref[...] - u_ref[...]))


def third_kernel(core_ref, lo_ref, lx_ref, acc_ref, u_ref, *refs):
    parts, out_ref, sum_ref = refs[:-2], refs[-2], refs[-1]
    s = functools.reduce(jnp.add, [p[...] for p in parts])
    sum_ref[...] = s
    out_ref[...] = acc_ref[...] - u_ref[...] - product(Pair(core_ref, lo_ref, lx_ref)[1], joined(s))


def both_ways(even, x, one_ref, two_ref):
    low, high = packed(x, 0), packed(x, 1)
    one_ref[...] = jnp.where(even, low, high)
    two_ref[...] = jnp.where(even, high, low)


def pair_kernel(
    core_ref, even_ref, io_ref, ix_ref, lo_ref, lx_ref, qo_ref, qx_ref, a_ref, b_ref, one_ref, two_ref, p_ref, q_ref
):
    even = even_ref[0] == 1
    inverse, below = Pair(core_ref, io_ref, ix_ref), Pair(core_ref, lo_ref, lx_ref)
    a, b = a_ref[...], b_ref[...]
    s_p = product(inverse[0], joined(jnp.where(even, a, b)))
    cat = joined(s_p)
    s_q = product(inverse[1], joined(jnp.where(even, b, a) - stacked(core_ref, qo_ref, qx_ref, cat)))
    both_ways(even, -product(below[0], cat) - product(below[1], joined(s_q)), one_ref, two_ref)
    p_ref[...] = s_p
    q_ref[...] = s_q


def less_kernel(core_ref, even_ref, lo_ref, lx_ref, p_ref, q_ref, acc_ref, one_ref, two_ref):
    below = Pair(core_ref, lo_ref, lx_ref)
    part = product(below[0], joined(p_ref[...])) + product(below[1], joined(q_ref[...]))
    both_ways(even_ref[0] == 1, acc_ref[...] - part, one_ref, two_ref)


def merge_kernel(own_ref, x_ref, y_ref, mine_ref, out_ref):
    out_ref[...] = x_ref[...] + y_ref[...] + mine_ref[...] * own_ref[0].astype(F32)


def final_kernel(
    core_ref, even_ref, io_ref, ix_ref, qo_ref, qx_ref, a_ref, b_ref, c_ref, d_ref, *refs
):
    known, out_ref = refs[:-1], refs[-1]
    even = even_ref[0] == 1
    inverse = Pair(core_ref, io_ref, ix_ref)
    one, two = a_ref[...] + c_ref[...], b_ref[...] + d_ref[...]
    s_p = product(inverse[0], joined(unpacked(jnp.where(even, one, two))))
    rest = unpacked(jnp.where(even, two, one)) - stacked(core_ref, qo_ref, qx_ref, joined(s_p))
    s_q = product(inverse[1], joined(rest))
    n = s_p.shape[0] // 2
    for slot, s in ((0, s_p), (1, s_q)):
        old = functools.reduce(jnp.add, [k[...] for k in known[slot::2]])
        old = jnp.where(even, packed(old, 0), packed(old, 1))
        out_ref[slot] = old + jnp.concatenate([s[:n], s[n:]], axis=1)


def update_kernel(core_ref, keep_ref, o0_ref, x0_ref, o1_ref, x1_ref, s_ref, out_ref, solved_ref):
    parts, _, rows, width = out_ref.shape
    steps, cuts = s_ref.shape[0] // 2, s_ref.shape[1]
    for slot in range(2):
        sides = []
        for half in range(cuts):
            pieces = [s_ref[slot * steps + j, half] for j in range(steps)]
            sides.append(unpacked(jnp.concatenate(pieces, axis=0)))
        solved_ref[slot] = jnp.concatenate(sides, axis=1)
    cats = [joined(solved_ref[slot]) for slot in range(2)]
    for a, w in enumerate((Pair(core_ref, o0_ref, x0_ref), Pair(core_ref, o1_ref, x1_ref))):
        terms = [product(w[slot], cats[slot]) for slot in range(2)]
        if a == 0:
            terms = [t * keep_ref[slot] for slot, t in enumerate(terms)]
        total = terms[0] + terms[1]
        for j in range(parts):
            out_ref[j, a] = total[j * rows : (j + 1) * rows]


def shards(panel, right_side, inverse_blocks):
    block = panel.shape[2]
    width = right_side.shape[3] // 2
    my_row, my_col = lax.axis_index("row"), lax.axis_index("col")
    row_count, col_count = lax.axis_size("row"), lax.axis_size("col")
    planes = row_count // 2
    plane, core = my_row // 2, my_row % 2

    def flag(condition):
        return jnp.asarray(condition).astype(jnp.int32).reshape(1)

    core_arg, even, zero = flag(core), flag(my_col % 2 == 0), flag(False)
    not_3, own_flag = flag(my_col != 3), flag((plane == 3) & (my_col == 7))
    keep = (my_col > 2 * plane + jnp.arange(2)).astype(F32)
    root = jnp.where(plane == 3, 6, 2 * plane + 2)
    share = block // row_count
    first_column, first_row = core * width, my_row * share
    (panel, core_arg, even, zero, not_3, own_flag, keep, root, first_column, first_row) = lax.optimization_barrier(
        (panel, core_arg, even, zero, not_3, own_flag, keep, root, first_column, first_row)
    )
    whole = ((block, width), F32)
    slim = ((block // 2, width), F32)

    def send(array, moves):
        pairs = [
            ((2 * a + h) * col_count + b, (2 * c + h) * col_count + d)
            for (a, b), (c, d) in moves
            for h in range(2)
        ]
        return lax.ppermute(array, BOTH, pairs)

    def swap(array):
        return lax.ppermute(array, "row", [(r, r ^ 1) for r in range(row_count)])

    inverse = inverse_blocks[0]
    rhs = lax.dynamic_slice(right_side, (0, 0, 0, first_column), (1, 1, block, width)).reshape(block, width)
    near = send(rhs, [((0, 0), (0, 1)), ((1, 0), (0, 2)), ((3, 0), (0, 3))])
    tile = retile(after(panel, rhs), 0)
    inverses = (inverse, swap(inverse))
    belows = (tile, swap(tile))
    far = send(after(rhs, tile), [((z, 0), (0, 4 + z)) for z in range(4)])

    def solve_first(choice, a, b, c):
        specs = [SMEM] * 2 + [VMEM] * 7
        return call(first_kernel, "first", 2, [whole] * 2, specs, core_arg, choice, *inverses, *belows, a, b, c)

    def solve_second(r, u):
        return call(second_kernel, "second", 1, [whole], [SMEM] + [VMEM] * 4, core_arg, *inverses, r, u)[0]

    def subtract(acc, u, *parts):
        specs = [SMEM] + [VMEM] * (4 + len(parts))
        return call(third_kernel, "third", 1, [whole] * 2, specs, core_arg, *belows, acc, u, *parts)

    p_0, u = solve_first(zero, near, far, far)
    s_q = solve_second(rhs, u)
    to_2 = send(s_q, [((0, 1), (0, 2))])
    to_3 = send(s_q, [((0, 1), (0, 3))])

    half_shape = ((block // 2, block), F32)
    (ahead,) = call(cut_kernel, "cut", 0, [half_shape], [SMEM] + [VMEM] * 2, core_arg, tile, after(belows[1], s_q))
    x = send(ahead, [((2, 5), (2, 6)), ((3, 7), (3, 6))])
    y = send(ahead, [((2, 5), (2, 7))])

    soon, q_0 = subtract(rhs, u, after(to_2, ahead), to_3)
    a = send(soon, [((0, 2), (1, 3))])
    b = send(soon, [((0, 3), (1, 3)), ((0, 2), (1, 4))])
    c = send(soon, [((0, 2), (1, 5))])
    late_5 = send(after(s_q, soon), [((0, 1), (0, 5))])
    late_4 = send(after(s_q, soon), [((0, 1), (0, 4))])
    late_6 = send(q_0, [((0, 2), (0, 6)), ((0, 3), (0, 7))])
    later, _ = subtract(rhs, u, late_4, late_5, late_6)
    acc = send(later, [((0, c), (1, c)) for c in range(4, 8)])

    (got,) = call(
        merge_kernel, "merge", 0, [half_shape], [SMEM] + [VMEM] * 3, own_flag, after(x, soon), y, ahead
    )
    coupling = (got, swap(got))

    a = after(a, got)
    p_1, u = solve_first(not_3, a, b, c)
    s_q = solve_second(b, u)
    to_4 = send(s_q, [((1, 3), (1, 4))])
    to_5 = send(s_q, [((1, 3), (1, 5))])
    soon, q_1 = subtract(acc, u, to_4, to_5)
    a = send(soon, [((1, 4), (2, 6)), ((1, 5), (2, 7))])
    b = send(soon, [((1, 4), (2, 7)), ((1, 5), (2, 6))])
    late = [send(s, [((1, 4), (1, 6)), ((1, 5), (1, 7))]) for s in (p_1, q_1)]
    specs = [SMEM] * 2 + [VMEM] * 5
    one, two = call(less_kernel, "less", 2, [slim] * 2, specs, core_arg, even, *belows, *late, acc)
    c = send(one, [((1, 6), (3, 6)), ((1, 7), (3, 7))])
    d = send(two, [((1, 6), (3, 7)), ((1, 7), (3, 6))])

    specs = [SMEM] * 2 + [VMEM] * 8
    outs = [slim] * 2 + [whole] * 2
    one, two, p_2, q_2 = call(
        pair_kernel, "pair", 5, outs, specs, core_arg, even, *inverses, *belows, *coupling, a, b
    )
    a = send(one, [((2, 6), (3, 6)), ((2, 7), (3, 7))])
    b = send(two, [((2, 6), (3, 7)), ((2, 7), (3, 6))])

    specs = [SMEM] * 2 + [VMEM] * 14
    known = (p_0, q_0, p_1, q_1, p_2, q_2)
    outs = [((2, block // 2, width), F32)]
    (mine,) = call(
        final_kernel, "final", 3, outs, specs, core_arg, even, *inverses, *coupling, a, b, c, d, *known
    )

    tile = retile(after(panel, mine), 1)
    cut = block // col_count
    pieces = lax.all_to_all(mine.reshape(col_count, cut, width), "col", 0, 0)
    piece = lax.dynamic_slice_in_dim(pieces, root, 2, 0)
    pieces = lax.all_to_all(jnp.broadcast_to(piece[None], (col_count, 2, cut, width)), "col", 0, 0)

    outs = [((row_count, 2, share, width), F32), ((2, block, width), F32)]
    specs = [SMEM] * 2 + [VMEM] * 5
    parts, mine = call(update_kernel, "update", 4, outs, specs, core_arg, keep, *belows, tile, swap(tile), pieces)
    parts = lax.all_to_all(parts, "row", 0, 0)
    sums = parts.reshape(planes, 2, 2, share, width).sum(0)
    sums = jnp.concatenate([sums[0], sums[1]], axis=-1)
    own = lax.dynamic_slice_in_dim(right_side, first_row, share, 2).reshape(2, share, 2 * width)
    updated = (own - sums).reshape(2, 1, share, 2 * width)

    ours = jnp.where(core == 0, mine[0], mine[1])
    theirs = swap(jnp.where(core == 0, mine[1], mine[0]))
    solved = jnp.concatenate([jnp.where(core == 0, ours, theirs), jnp.where(core == 0, theirs, ours)], axis=1)
    return solved.reshape(1, block, 2 * width), updated


def solution(mesh):
    placed = (P(None, "col", None, "row", None), P(None, "col", None, None), P("row", None, None))
    return jax.shard_map(
        shards,
        mesh=mesh,
        in_specs=placed,
        out_specs=(P("row", None, None), P(None, "col", "row", None)),
        check_vma=False,
    )
```

```python
import functools

import jax
import jax.numpy as jnp
from jax import lax
from jax.experimental import pallas as pl
from jax.experimental.pallas import tpu as pltpu
from jax.sharding import PartitionSpec as P

F32 = jnp.float32
BF16 = jnp.bfloat16
LIMIT = 12 * 1024 * 1024
MOST = 56 * 1024 * 1024
BOTH = ("row", "col")
VMEM = pl.BlockSpec(memory_space=pltpu.VMEM)
SMEM = pl.BlockSpec(memory_space=pltpu.SMEM)
ANY = pl.BlockSpec(memory_space=pl.ANY)


def halves(x):
    hi = x.astype(BF16)
    return hi, (x - hi.astype(F32)).astype(BF16)


def joined(x):
    return jnp.concatenate(halves(x), axis=1)


def product(w, cat):
    width = cat.shape[1] // 2
    hi, lo = halves(w)
    one = jnp.dot(hi, cat, preferred_element_type=F32)
    two = jnp.dot(lo, cat[:, :width], preferred_element_type=F32)
    return one[:, :width] + one[:, width:] + two


class Pair:
    def __init__(self, core_ref, own_ref, other_ref):
        self.first, self.refs = core_ref[0] == 0, (own_ref, other_ref)

    def __getitem__(self, slot):
        own, other = (ref[...] for ref in self.refs)
        return jnp.where(self.first, own, other) if slot == 0 else jnp.where(self.first, other, own)


def stacked(core_ref, own_ref, other_ref, cat):
    first = core_ref[0] == 0
    own, other = product(own_ref[...], cat), product(other_ref[...], cat)
    return jnp.concatenate([jnp.where(first, own, other), jnp.where(first, other, own)], axis=0)


def packed(x, half):
    n, width = x.shape
    part = x[:, half * width // 2 : (half + 1) * width // 2]
    return jnp.concatenate([part[: n // 2], part[n // 2 :]], axis=1)


def unpacked(x):
    width = x.shape[1] // 2
    return jnp.concatenate([x[:, :width], x[:, width:]], axis=0)


def cost(flops, nbytes):
    return pl.CostEstimate(flops=flops, bytes_accessed=nbytes, transcendentals=0)


def call(kernel, name, products, outs, specs, *args, scratch=(), limit=LIMIT):
    n = 1024
    return pl.pallas_call(
        kernel,
        out_shape=tuple(jax.ShapeDtypeStruct(shape, kind) for shape, kind in outs),
        in_specs=specs,
        out_specs=(VMEM,) * len(outs),
        scratch_shapes=scratch,
        compiler_params=pltpu.CompilerParams(vmem_limit_bytes=limit),
        cost_estimate=cost(6 * products * n * n * 128, 4 * products * n * n),
        name=name,
    )(*args)


def after(x, *others):
    return lax.optimization_barrier((x,) + others)[0]


def retile_kernel(a, panel_ref, out_ref, sem):
    copy = pltpu.make_async_copy(panel_ref.at[a, 0, :, 0], out_ref, sem.at[0])
    copy.start()
    copy.wait()


def retile(panel, a):
    n, depth = panel.shape[2], panel.shape[4]
    return pl.pallas_call(
        functools.partial(retile_kernel, a),
        out_shape=jax.ShapeDtypeStruct((n, depth), F32),
        in_specs=[pl.BlockSpec(memory_space=pltpu.HBM)],
        out_specs=VMEM,
        scratch_shapes=[pltpu.SemaphoreType.DMA((1,))],
        compiler_params=pltpu.CompilerParams(vmem_limit_bytes=LIMIT if a else MOST),
        cost_estimate=cost(0, 8 * n * depth),
        name="retile",
    )(panel)


def head_rows(cuts):
    def kernel(column_ref, right_ref, rhs_ref, *refs):
        parts, sem = refs[:-1], refs[-1]
        width = rhs_ref.shape[1]
        columns = pl.ds(pl.multiple_of(column_ref[0], width), width)
        copies = [pltpu.make_async_copy(right_ref.at[0, 0, :, columns], rhs_ref, sem.at[0])]
        for i, part in enumerate(parts):
            rows = pl.ds(cuts[i], cuts[i + 1] - cuts[i])
            copies.append(pltpu.make_async_copy(right_ref.at[0, 0, rows, columns], part, sem.at[i + 1]))
        for copy in copies:
            copy.start()
        for copy in copies:
            copy.wait()

    return kernel


def cut_kernel(core_ref, own_ref, other_ref, out_ref):
    n = out_ref.shape[0]

    @pl.when(core_ref[0] == 0)
    def _():
        out_ref[...] = own_ref[:n]

    @pl.when(core_ref[0] == 1)
    def _():
        out_ref[...] = other_ref[n:]


def first_kernel(core_ref, io_ref, ix_ref, lo_ref, lx_ref, *refs):
    parts, s_ref, u_ref = refs[:-2], refs[-2], refs[-1]
    r = functools.reduce(jnp.add, [p[...] for p in parts])
    s = product(Pair(core_ref, io_ref, ix_ref)[0], joined(r))
    s_ref[...] = s
    u_ref[...] = product(Pair(core_ref, lo_ref, lx_ref)[0], joined(s))


def head_kernel(core_ref, io_ref, ix_ref, lo_ref, lx_ref, x_ref, y_ref, z_ref, s_ref, u_ref):
    r = jnp.concatenate([x_ref[...], y_ref[...], z_ref[...]], axis=0)
    s = product(Pair(core_ref, io_ref, ix_ref)[0], joined(r))
    s_ref[...] = s
    u_ref[...] = product(Pair(core_ref, lo_ref, lx_ref)[0], joined(s))


def second_kernel(core_ref, io_ref, ix_ref, r_ref, u_ref, s_ref):
    s_ref[...] = product(Pair(core_ref, io_ref, ix_ref)[1], joined(r_ref[...] - u_ref[...]))


def third_kernel(core_ref, lo_ref, lx_ref, acc_ref, u_ref, *refs):
    parts, out_ref, sum_ref = refs[:-2], refs[-2], refs[-1]
    s = functools.reduce(jnp.add, [p[...] for p in parts])
    sum_ref[...] = s
    out_ref[...] = acc_ref[...] - u_ref[...] - product(Pair(core_ref, lo_ref, lx_ref)[1], joined(s))


def both_ways(even, x, one_ref, two_ref):
    low, high = packed(x, 0), packed(x, 1)
    one_ref[...] = jnp.where(even, low, high)
    two_ref[...] = jnp.where(even, high, low)


def pair_kernel(
    core_ref, even_ref, io_ref, ix_ref, lo_ref, lx_ref, qo_ref, qx_ref, a_ref, b_ref, one_ref, two_ref, p_ref, q_ref
):
    even = even_ref[0] == 1
    inverse, below = Pair(core_ref, io_ref, ix_ref), Pair(core_ref, lo_ref, lx_ref)
    a, b = a_ref[...], b_ref[...]
    s_p = product(inverse[0], joined(jnp.where(even, a, b)))
    cat = joined(s_p)
    s_q = product(inverse[1], joined(jnp.where(even, b, a) - stacked(core_ref, qo_ref, qx_ref, cat)))
    both_ways(even, -product(below[0], cat) - product(below[1], joined(s_q)), one_ref, two_ref)
    p_ref[...] = s_p
    q_ref[...] = s_q


def less_kernel(core_ref, even_ref, lo_ref, lx_ref, acc_ref, u_ref, x_ref, y_ref, one_ref, two_ref):
    part = product(Pair(core_ref, lo_ref, lx_ref)[1], joined(x_ref[...] + y_ref[...]))
    both_ways(even_ref[0] == 1, acc_ref[...] - u_ref[...] - part, one_ref, two_ref)


def merge_kernel(own_ref, x_ref, y_ref, mine_ref, out_ref):
    out_ref[...] = x_ref[...] + y_ref[...] + mine_ref[...] * own_ref[0].astype(F32)


def final_kernel(
    core_ref, even_ref, io_ref, ix_ref, qo_ref, qx_ref, a_ref, b_ref, c_ref, d_ref, *refs
):
    known, out_ref = refs[:-1], refs[-1]
    even = even_ref[0] == 1
    inverse = Pair(core_ref, io_ref, ix_ref)
    one, two = a_ref[...] + c_ref[...], b_ref[...] + d_ref[...]
    s_p = product(inverse[0], joined(unpacked(jnp.where(even, one, two))))
    rest = unpacked(jnp.where(even, two, one)) - stacked(core_ref, qo_ref, qx_ref, joined(s_p))
    s_q = product(inverse[1], joined(rest))
    n = s_p.shape[0] // 2
    for slot, s in ((0, s_p), (1, s_q)):
        old = functools.reduce(jnp.add, [k[...] for k in known[slot::2]])
        old = jnp.where(even, packed(old, 0), packed(old, 1))
        out_ref[slot] = old + jnp.concatenate([s[:n], s[n:]], axis=1)


def finish_kernel(core_ref, ours_ref, theirs_ref, out_ref):
    first = core_ref[0] == 0
    ours, theirs = ours_ref[...], theirs_ref[...]
    width = ours.shape[1]
    out_ref[0, :, :width] = jnp.where(first, ours, theirs)
    out_ref[0, :, width:] = jnp.where(first, theirs, ours)


def spread_kernel(root_ref, pieces_ref, out_ref):
    piece = pieces_ref[pl.ds(root_ref[0], 2)]
    for j in range(out_ref.shape[0]):
        out_ref[j] = piece


def combine_kernel(row_ref, parts_ref, right_ref, out_ref, own_ref, sem):
    share, width = parts_ref.shape[2:]
    rows = pl.ds(pl.multiple_of(row_ref[0], share), share)
    copy = pltpu.make_async_copy(right_ref.at[:, 0, rows, :], own_ref, sem.at[0])
    copy.start()
    sums = [functools.reduce(jnp.add, [parts_ref[2 * z + h] for z in range(parts_ref.shape[0] // 2)]) for h in range(2)]
    copy.wait()
    for h in range(2):
        columns = slice(h * width, (h + 1) * width)
        out_ref[:, 0, :, columns] = own_ref[:, :, columns] - sums[h]


def update_kernel(core_ref, keep_ref, o0_ref, x0_ref, o1_ref, x1_ref, s_ref, out_ref, ours_ref, theirs_ref, solved_ref):
    parts, _, rows, width = out_ref.shape
    steps, cuts = s_ref.shape[0] // 2, s_ref.shape[1]
    for slot in range(2):
        sides = []
        for half in range(cuts):
            pieces = [s_ref[slot * steps + j, half] for j in range(steps)]
            sides.append(unpacked(jnp.concatenate(pieces, axis=0)))
        solved_ref[slot] = jnp.concatenate(sides, axis=1)
    first = core_ref[0] == 0
    ours_ref[...] = jnp.where(first, solved_ref[0], solved_ref[1])
    theirs_ref[...] = jnp.where(first, solved_ref[1], solved_ref[0])
    cats = [joined(solved_ref[slot]) for slot in range(2)]
    for a, w in enumerate((Pair(core_ref, o0_ref, x0_ref), Pair(core_ref, o1_ref, x1_ref))):
        terms = [product(w[slot], cats[slot]) for slot in range(2)]
        if a == 0:
            terms = [t * keep_ref[slot] for slot, t in enumerate(terms)]
        total = terms[0] + terms[1]
        for j in range(parts):
            out_ref[j, a] = total[j * rows : (j + 1) * rows]


def shards(panel, right_side, inverse_blocks):
    block = panel.shape[2]
    width = right_side.shape[3] // 2
    my_row, my_col = lax.axis_index("row"), lax.axis_index("col")
    row_count, col_count = lax.axis_size("row"), lax.axis_size("col")
    planes = row_count // 2
    plane, core = my_row // 2, my_row % 2

    def flag(condition):
        return jnp.asarray(condition).astype(jnp.int32).reshape(1)

    core_arg, even = flag(core), flag(my_col % 2 == 0)
    own_flag = flag((plane == 3) & (my_col == 7))
    keep = (my_col > 2 * plane + jnp.arange(2)).astype(F32)
    root = flag(jnp.where(plane == 3, 6, 2 * plane + 2))
    share = block // row_count
    first_column, first_row = flag(core * width), flag(my_row * share)
    (panel, core_arg, even, own_flag, keep, root, first_column, first_row) = lax.optimization_barrier(
        (panel, core_arg, even, own_flag, keep, root, first_column, first_row)
    )
    whole = ((block, width), F32)
    slim = ((block // 2, width), F32)

    def send(array, moves):
        pairs = [
            ((2 * a + h) * col_count + b, (2 * c + h) * col_count + d)
            for (a, b), (c, d) in moves
            for h in range(2)
        ]
        return lax.ppermute(array, BOTH, pairs)

    def swap(array):
        return lax.ppermute(array, "row", [(r, r ^ 1) for r in range(row_count)])

    inverse = inverse_blocks[0]
    cuts = (0, 384, 704, 1024)
    outs = [whole] + [((cuts[i + 1] - cuts[i], width), F32) for i in range(3)]
    scratch = [pltpu.SemaphoreType.DMA((4,))]
    rhs, *thirds = call(head_rows(cuts), "rhs", 0, outs, [SMEM, ANY], first_column, right_side, scratch=scratch, limit=MOST)
    soonest = [send(part, [((z, 0), (0, 1))]) for part, z in zip(thirds, (0, 1, 3))]
    near = send(rhs, [((1, 0), (0, 2)), ((3, 0), (0, 3))])
    tile = retile(after(panel, rhs), 0)
    inverses = (inverse, swap(inverse))
    belows = (tile, swap(tile))
    far = send(after(rhs, tile), [((z, 0), (0, 4 + z)) for z in range(4)])

    def solve_first(kernel, *parts):
        specs = [SMEM] + [VMEM] * (4 + len(parts))
        return call(kernel, "first", 2, [whole] * 2, specs, core_arg, *inverses, *belows, *parts)

    def solve_second(r, u):
        return call(second_kernel, "second", 1, [whole], [SMEM] + [VMEM] * 4, core_arg, *inverses, r, u)[0]

    def subtract(acc, u, *parts):
        specs = [SMEM] + [VMEM] * (4 + len(parts))
        return call(third_kernel, "third", 1, [whole] * 2, specs, core_arg, *belows, acc, u, *parts)

    _, u = solve_first(head_kernel, *soonest)
    s_q = solve_second(rhs, u)
    to_2 = send(s_q, [((0, 1), (0, 2))])
    to_3 = send(s_q, [((0, 1), (0, 3))])
    p_0, u = solve_first(first_kernel, after(near, s_q), far)

    half_shape = ((block // 2, block), F32)
    (ahead,) = call(cut_kernel, "cut", 0, [half_shape], [SMEM] + [VMEM] * 2, core_arg, *belows)
    ahead_on = after(ahead, p_0)
    x = send(ahead_on, [((2, 5), (2, 6)), ((3, 7), (3, 6))])
    y = send(ahead_on, [((2, 5), (2, 7))])

    soon, q_0 = subtract(rhs, u, to_2, to_3)
    a = send(soon, [((0, 2), (1, 3))])
    r_q = send(soon, [((0, 3), (1, 3))])
    b = send(soon, [((0, 2), (1, 4))])
    c = send(soon, [((0, 2), (1, 5))])

    late_5 = send(s_q, [((0, 1), (0, 5))])
    late_4 = send(s_q, [((0, 1), (0, 4))])
    later, _ = subtract(rhs, u, after(late_4, soon), late_5)
    acc = send(later, [((0, c), (1, c)) for c in (4, 5)])

    _, u_1 = solve_first(first_kernel, after(a, later))
    s_1 = solve_second(r_q, u_1)
    to_4 = send(s_1, [((1, 3), (1, 4))])
    to_5 = send(s_1, [((1, 3), (1, 5))])
    b = after(b, s_1)
    d_6 = send(soon, [((0, 2), (1, 6))])
    d_7 = send(soon, [((0, 2), (1, 7))])
    p_1, u_1 = solve_first(first_kernel, b, c, d_6, d_7)
    to_6 = send(after(s_1, p_1), [((1, 3), (1, 6))])
    to_7 = send(after(s_1, p_1), [((1, 3), (1, 7))])

    soon_1, q_1 = subtract(acc, u_1, to_4, to_5)
    a = send(soon_1, [((1, 4), (2, 6)), ((1, 5), (2, 7))])
    b = send(soon_1, [((1, 4), (2, 7)), ((1, 5), (2, 6))])

    specs = [SMEM] + [VMEM] * 3
    (got,) = call(merge_kernel, "merge", 0, [half_shape], specs, own_flag, after(x, soon_1), y, ahead)
    coupling = (got, swap(got))

    late_6 = send(after(q_0, p_1), [((0, 2), (0, 6)), ((0, 3), (0, 7))])
    later, _ = subtract(rhs, u, after(late_6, soon_1))
    acc = send(later, [((0, c), (1, c)) for c in (6, 7)])
    specs = [SMEM] * 2 + [VMEM] * 6
    one, two = call(less_kernel, "less", 1, [slim] * 2, specs, core_arg, even, *belows, acc, u_1, to_6, to_7)
    c = send(one, [((1, 6), (3, 6)), ((1, 7), (3, 7))])
    d = send(two, [((1, 6), (3, 7)), ((1, 7), (3, 6))])

    specs = [SMEM] * 2 + [VMEM] * 8
    outs = [slim] * 2 + [whole] * 2
    one, two, p_2, q_2 = call(
        pair_kernel, "pair", 0, outs, specs, core_arg, even, *inverses, *belows, *coupling, a, b
    )
    a = send(one, [((2, 6), (3, 6)), ((2, 7), (3, 7))])
    b = send(two, [((2, 6), (3, 7)), ((2, 7), (3, 6))])

    specs = [SMEM] * 2 + [VMEM] * 14
    known = (p_0, q_0, p_1, q_1, p_2, q_2)
    outs = [((2, block // 2, width), F32)]
    (mine,) = call(
        final_kernel, "final", 3, outs, specs, core_arg, even, *inverses, *coupling, a, b, c, d, *known
    )

    cut = block // col_count
    pieces = lax.all_to_all(mine.reshape(col_count, cut, width), "col", 0, 0)
    outs = [((col_count, 2, cut, width), F32)]
    (spread,) = call(spread_kernel, "spread", 0, outs, [SMEM, VMEM], root, pieces)
    tile_1 = retile(after(panel, spread), 1)
    other_1 = swap(tile_1)
    pieces = lax.all_to_all(spread, "col", 0, 0)

    outs = [((row_count, 2, share, width), F32)] + [whole] * 2
    specs = [SMEM] * 2 + [VMEM] * 5
    scratch = [pltpu.VMEM((2, block, width), F32)]
    parts, ours, theirs = call(
        update_kernel, "update", 4, outs, specs, core_arg, keep, *belows, tile_1, other_1, pieces, scratch=scratch
    )
    parts = lax.all_to_all(parts, "row", 0, 0)
    scratch = [pltpu.VMEM((2, share, 2 * width), F32), pltpu.SemaphoreType.DMA((1,))]
    outs = [((2, 1, share, 2 * width), F32)]
    (updated,) = call(combine_kernel, "combine", 0, outs, [SMEM, VMEM, ANY], first_row, parts, right_side, scratch=scratch)

    outs = [((1, block, 2 * width), F32)]
    (solved,) = call(finish_kernel, "finish", 0, outs, [SMEM] + [VMEM] * 2, core_arg, ours, swap(theirs))
    return solved, updated


def solution(mesh):
    placed = (P(None, "col", None, "row", None), P(None, "col", None, None), P("row", None, None))
    return jax.shard_map(
        shards,
        mesh=mesh,
        in_specs=placed,
        out_specs=(P("row", None, None), P(None, "col", "row", None)),
        check_vma=False,
    )
```

```python
import functools

import jax
import jax.numpy as jnp
from jax import lax
from jax.experimental import pallas as pl
from jax.experimental.pallas import tpu as pltpu
from jax.sharding import PartitionSpec as P

F32 = jnp.float32
BF16 = jnp.bfloat16
LIMIT = 12 * 1024 * 1024
BOTH = ("row", "col")
VMEM = pl.BlockSpec(memory_space=pltpu.VMEM)
SMEM = pl.BlockSpec(memory_space=pltpu.SMEM)
ANY = pl.BlockSpec(memory_space=pl.ANY)


def halves(x):
    hi = x.astype(BF16)
    return hi, (x - hi.astype(F32)).astype(BF16)


def joined(x):
    return jnp.concatenate(halves(x), axis=1)


def product(w, cat):
    n, width = cat.shape[0], cat.shape[1] // 2
    tiles = []
    for i in range(4):
        hi, lo = halves(w(slice(i * n // 4, (i + 1) * n // 4)))
        one = jnp.dot(hi, cat, preferred_element_type=F32)
        two = jnp.dot(lo, cat[:, :width], preferred_element_type=F32)
        tiles.append(one[:, :width] + one[:, width:] + two)
    return jnp.concatenate(tiles, axis=0)


class Pair:
    def __init__(self, ctl, own_ref, other_ref):
        self.first, self.refs = ctl["core"] == 0, (own_ref, other_ref)

    def __getitem__(self, slot):
        def rows(at):
            own, other = (ref[at, :] for ref in self.refs)
            return jnp.where(self.first, own, other) if slot == 0 else jnp.where(self.first, other, own)

        return rows


def packed(x, half):
    n, width = x.shape
    part = x[:, half * width // 2 : (half + 1) * width // 2]
    return jnp.concatenate([part[: n // 2], part[n // 2 :]], axis=1)


def unpacked(x):
    width = x.shape[1] // 2
    return jnp.concatenate([x[:, :width], x[:, width:]], axis=0)


def cost(flops, nbytes):
    return pl.CostEstimate(flops=flops, bytes_accessed=nbytes, transcendentals=0)


class Words:
    def __init__(self, names, refs):
        self.refs = dict(zip(names, refs))

    def __getitem__(self, name):
        return self.refs[name][0]


def call(kernel, name, words, outs, specs, *args, scratch=(), to=VMEM):
    def body(*refs):
        kernel(Words(words, refs), *refs[len(words) :])

    return pl.pallas_call(
        body,
        out_shape=tuple(jax.ShapeDtypeStruct(shape, kind) for shape, kind in outs),
        in_specs=[SMEM] * len(words) + specs,
        out_specs=(to,) * len(outs),
        scratch_shapes=scratch,
        compiler_params=pltpu.CompilerParams(vmem_limit_bytes=LIMIT),
        cost_estimate=cost(0, 0),
        name=name,
    )(*words.values(), *args)


def only(ctl, who, outs, body):
    pl.when(ctl[who] == 1)(body)

    @pl.when(ctl[who] == 0)
    def _():
        for ref in outs:
            ref[...] = jnp.zeros_like(ref)


def after(x, *others):
    return lax.optimization_barrier((x,) + others)[0]


def retile_kernel(a, panel_ref, out_ref, sem):
    copy = pltpu.make_async_copy(panel_ref.at[a, 0, :, 0], out_ref, sem.at[0])
    copy.start()
    copy.wait()


def retile(panel, a):
    n, depth = panel.shape[2], panel.shape[4]
    return pl.pallas_call(
        functools.partial(retile_kernel, a),
        out_shape=jax.ShapeDtypeStruct((n, depth), F32),
        in_specs=[pl.BlockSpec(memory_space=pltpu.HBM)],
        out_specs=VMEM,
        scratch_shapes=[pltpu.SemaphoreType.DMA((1,))],
        compiler_params=pltpu.CompilerParams(vmem_limit_bytes=42 * 1024 * 1024),
        cost_estimate=cost(0, 0),
        name="retile",
    )(panel)


def rhs_kernel(ctl, right_ref, rhs_ref, low_ref, high_ref, sem):
    n, width = rhs_ref.shape
    columns = pl.ds(pl.multiple_of(ctl["column"], width), width)
    copies = [
        pltpu.make_async_copy(right_ref.at[0, 0, rows, columns], ref, sem.at[i])
        for i, (rows, ref) in enumerate(
            ((pl.ds(0, n), rhs_ref), (pl.ds(0, n // 2), low_ref), (pl.ds(n // 2, n // 2), high_ref))
        )
    ]
    for copy in copies:
        copy.start()
    for copy in copies:
        copy.wait()


def cut_kernel(ctl, own_ref, other_ref, out_ref, sem):
    for core, ref in enumerate((own_ref, other_ref)):

        @pl.when((ctl["cut"] == 1) & (ctl["core"] == core))
        def _():
            copy = pltpu.make_async_copy(ref, out_ref, sem.at[0])
            copy.start()
            copy.wait()


def first_kernel(halves_given, ctl, io_ref, ix_ref, lo_ref, lx_ref, *refs):
    parts, s_ref, u_ref = refs[:-2], refs[-2], refs[-1]
    values = [p[...] for p in parts]
    r = jnp.concatenate(values, axis=0) if halves_given else functools.reduce(jnp.add, values)
    s = product(Pair(ctl, io_ref, ix_ref)[0], joined(r))
    s_ref[...] = s
    u_ref[...] = product(Pair(ctl, lo_ref, lx_ref)[0], joined(s))


def second_kernel(ctl, io_ref, ix_ref, r_ref, u_ref, s_ref):
    s_ref[...] = product(Pair(ctl, io_ref, ix_ref)[1], joined(r_ref[...] - u_ref[...]))


def third_kernel(ctl, lo_ref, lx_ref, acc_ref, u_ref, x_ref, y_ref, out_ref, sum_ref):
    s = x_ref[...] + y_ref[...]
    sum_ref[...] = s
    out_ref[...] = acc_ref[...] - u_ref[...] - product(Pair(ctl, lo_ref, lx_ref)[1], joined(s))


def later_kernel(ctl, lo_ref, lx_ref, acc_ref, u_ref, v_ref, *refs):
    parts, out_ref = refs[:-1], refs[-1]

    def body():
        s = functools.reduce(jnp.add, [p[...] for p in parts])
        u = u_ref[...] + v_ref[...]
        out_ref[...] = acc_ref[...] - u - product(Pair(ctl, lo_ref, lx_ref)[1], joined(s))

    only(ctl, "late", (out_ref,), body)


def both_ways(even, x, one_ref, two_ref):
    low, high = packed(x, 0), packed(x, 1)
    one_ref[...] = jnp.where(even, low, high)
    two_ref[...] = jnp.where(even, high, low)


def pair_kernel(
    ctl, io_ref, ix_ref, lo_ref, lx_ref, qo_ref, qx_ref, a_ref, b_ref, one_ref, two_ref, p_ref, q_ref
):
    even = ctl["even"] == 1
    inverse, below = Pair(ctl, io_ref, ix_ref), Pair(ctl, lo_ref, lx_ref)
    a, b = a_ref[...], b_ref[...]
    s_p = product(inverse[0], joined(jnp.where(even, a, b)))
    cat = joined(s_p)
    rest = jnp.where(even, b, a) - product(lambda at: qo_ref[at, :] + qx_ref[at, :], cat)
    s_q = product(inverse[1], joined(rest))
    both_ways(even, -product(below[0], cat) - product(below[1], joined(s_q)), one_ref, two_ref)
    p_ref[...] = s_p
    q_ref[...] = s_q


def less_kernel(ctl, io_ref, ix_ref, lo_ref, lx_ref, r_ref, t_ref, x_ref, y_ref, acc_ref, one_ref, two_ref):
    def body():
        below = Pair(ctl, lo_ref, lx_ref)
        s_p = product(Pair(ctl, io_ref, ix_ref)[0], joined(r_ref[...] + t_ref[...]))
        part = product(below[0], joined(s_p)) + product(below[1], joined(x_ref[...] + y_ref[...]))
        both_ways(ctl["even"] == 1, acc_ref[...] - part, one_ref, two_ref)

    only(ctl, "six", (one_ref, two_ref), body)


def known_kernel(ctl, *refs):
    known, out_ref = refs[:-1], refs[-1]
    for slot in range(2):
        s = functools.reduce(jnp.add, [k[...] for k in known[slot::2]])
        out_ref[slot] = jnp.where(ctl["even"] == 1, packed(s, 0), packed(s, 1))


def final_kernel(
    ctl, io_ref, ix_ref, lo_ref, lx_ref, qo_ref, qx_ref, a_ref, b_ref, c_ref, d_ref, known_ref, out_ref
):
    even = ctl["even"] == 1
    inverse, own = Pair(ctl, io_ref, ix_ref), Pair(ctl, lo_ref, lx_ref)[0]

    def coupling(at):
        return jnp.where(ctl["own"] == 1, own(at), qo_ref[at, :] + qx_ref[at, :])

    one, two = a_ref[...] + c_ref[...], b_ref[...] + d_ref[...]
    s_p = product(inverse[0], joined(unpacked(jnp.where(even, one, two))))
    rest = unpacked(jnp.where(even, two, one)) - product(coupling, joined(s_p))
    s_q = product(inverse[1], joined(rest))
    n = s_p.shape[0] // 2
    for slot, s in ((0, s_p), (1, s_q)):
        out_ref[slot] = known_ref[slot] + jnp.concatenate([s[:n], s[n:]], axis=1)


def spread_kernel(ctl, pieces_ref, out_ref):
    piece = pieces_ref[pl.ds(ctl["root"], 2)]
    for j in range(out_ref.shape[0]):
        out_ref[j] = piece


def gather_kernel(ctl, pieces_ref, solved_ref, theirs_ref):
    steps, cuts = pieces_ref.shape[0] // 2, pieces_ref.shape[1]
    for slot in range(2):
        sides = []
        for half in range(cuts):
            pieces = [pieces_ref[slot * steps + j, half] for j in range(steps)]
            sides.append(unpacked(jnp.concatenate(pieces, axis=0)))
        solved_ref[slot] = jnp.concatenate(sides, axis=1)
    theirs_ref[...] = jnp.where(ctl["core"] == 0, solved_ref[1], solved_ref[0])


def update_kernel(ctl, o0_ref, x0_ref, o1_ref, x1_ref, solved_ref, out_ref):
    parts, _, rows, width = out_ref.shape
    cats = [joined(solved_ref[slot]) for slot in range(2)]
    for a, w in enumerate((Pair(ctl, o0_ref, x0_ref), Pair(ctl, o1_ref, x1_ref))):
        terms = [product(w[slot], cats[slot]) for slot in range(2)]
        if a == 0:
            terms = [t * ctl[("keep_p", "keep_q")[slot]].astype(F32) for slot, t in enumerate(terms)]
        total = terms[0] + terms[1]
        for j in range(parts):
            out_ref[j, a] = total[j * rows : (j + 1) * rows]


def finish_kernel(ctl, solved_ref, theirs_ref, out_ref, sem):
    core, width = ctl["core"], theirs_ref.shape[1]
    copies = [
        pltpu.make_async_copy(ref, out_ref.at[0, :, pl.ds(pl.multiple_of(h * width, width), width)], sem.at[i])
        for i, (h, ref) in enumerate(((core, solved_ref.at[core]), (1 - core, theirs_ref)))
    ]
    for copy in copies:
        copy.start()
    for copy in copies:
        copy.wait()


def combine_kernel(ctl, parts_ref, right_ref, out_ref, own_ref, sem):
    share, width = parts_ref.shape[2:]
    rows = pl.ds(pl.multiple_of(ctl["row"], share), share)
    copy = pltpu.make_async_copy(right_ref.at[:, 0, rows, :], own_ref, sem.at[0])
    copy.start()
    sums = [functools.reduce(jnp.add, [parts_ref[2 * z + h] for z in range(parts_ref.shape[0] // 2)]) for h in range(2)]
    copy.wait()
    for h in range(2):
        columns = slice(h * width, (h + 1) * width)
        out_ref[:, 0, :, columns] = own_ref[:, :, columns] - sums[h]


def shards(panel, right_side, inverse_blocks):
    block = panel.shape[2]
    width = right_side.shape[3] // 2
    my_row, my_col = lax.axis_index("row"), lax.axis_index("col")
    row_count, col_count = lax.axis_size("row"), lax.axis_size("col")
    plane, core = my_row // 2, my_row % 2
    share = block // row_count
    whole, half, slim = (((rows, width), F32) for rows in (block, block // 2, block // 2))

    def at(z, low, high):
        return (plane == z) & (my_col >= low) & (my_col <= high)

    words = {
        "core": core,
        "even": my_col % 2 == 0,
        "column": core * width,
        "row": my_row * share,
        "root": jnp.where(plane == 3, 6, 2 * plane + 2),
        "keep_p": my_col > 2 * plane,
        "keep_q": my_col > 2 * plane + 1,
        "own": at(3, 7, 7),
        "cut": at(2, 5, 5) | at(3, 7, 7),
        "late": at(0, 4, 7),
        "six": at(1, 6, 7),
    }
    words = {name: jnp.asarray(word).astype(jnp.int32).reshape(1) for name, word in words.items()}
    panel, right_side, words = lax.optimization_barrier((panel, right_side, words))

    def pick(*names):
        return {name: words[name] for name in names}

    just_core = pick("core")

    def permute(array, moves):
        place = [[(2 * z + h) * col_count + c for z, h, c in ends] for ends in moves]
        return lax.ppermute(array, BOTH, [tuple(p) for p in place])

    def send(array, moves):
        return permute(array, [((a, h, b), (c, h, d)) for (a, b), (c, d) in moves for h in range(2)])

    def swap(array):
        return lax.ppermute(array, "row", [(r, r ^ 1) for r in range(row_count)])

    inverse = inverse_blocks[0]
    tile = retile(panel, 0)
    belows = (tile, swap(tile))
    inverses = (inverse, swap(inverse))
    scratch = [pltpu.SemaphoreType.DMA((3,))]
    outs = [whole, half, half]
    rhs, low, high = call(rhs_kernel, "rhs", pick("column"), outs, [ANY], after(right_side, tile), scratch=scratch)
    low_1 = send(low, [((0, 0), (0, 1)), ((1, 0), (0, 2)), ((3, 0), (0, 3)), ((2, 0), (0, 4))])
    high_1 = send(high, [((3, 0), (0, 1)), ((0, 0), (0, 2)), ((1, 0), (0, 3)), ((2, 0), (0, 4))])

    def solve_first(parts, halves_given=False):
        kernel = functools.partial(first_kernel, halves_given)
        return call(kernel, "first", just_core, [whole] * 2, [VMEM] * (4 + len(parts)), *inverses, *belows, *parts)

    def solve_second(r, u):
        return call(second_kernel, "second", just_core, [whole], [VMEM] * 4, *inverses, r, u)[0]

    def subtract(acc, u, x, y):
        return call(third_kernel, "third", just_core, [whole] * 2, [VMEM] * 6, *belows, acc, u, x, y)

    def subtract_late(acc, u, v, *parts):
        specs = [VMEM] * (5 + len(parts))
        return call(later_kernel, "later", pick("core", "late"), [whole], specs, *belows, acc, u, v, *parts)[0]

    p_0, u = solve_first((low_1, high_1), True)
    s_q = solve_second(rhs, u)
    to_2 = send(s_q, [((0, 1), (0, 2))])
    to_3 = send(s_q, [((0, 1), (0, 3))])
    low_2 = send(after(low, low_1), [((0, 0), (0, 5)), ((1, 0), (0, 6)), ((3, 0), (0, 7))])
    high_2 = send(after(high, low_1), [((1, 0), (0, 5)), ((3, 0), (0, 6)), ((0, 0), (0, 7))])
    _, v = solve_first((after(low_2, s_q), high_2), True)

    soon, q_0 = subtract(rhs, u, to_2, to_3)
    a = send(soon, [((0, 2), (1, 3))])
    b = send(soon, [((0, 3), (1, 3)), ((0, 2), (1, 4))])
    c = send(soon, [((0, 2), (1, 5))])

    late_5 = send(s_q, [((0, 1), (0, 5))])
    late_4 = send(s_q, [((0, 1), (0, 4))])
    later = subtract_late(rhs, u, v, after(late_5, soon), late_4)
    acc = send(later, [((0, c), (1, c)) for c in (4, 5)])

    outs = [((block, block), F32)]
    scratch = [pltpu.SemaphoreType.DMA((1,))]
    given = (tile, after(belows[1], later))
    (ahead,) = call(cut_kernel, "cut", pick("core", "cut"), outs, [ANY] * 2, *given, scratch=scratch)
    got = permute(ahead, [((2, 0, 5), (2, 0, 6)), ((2, 1, 5), (2, 1, 7)), ((3, 0, 7), (3, 0, 6))])

    _, u_1 = solve_first((after(a, later),))
    s_1 = solve_second(b, u_1)
    to_4 = send(s_1, [((1, 3), (1, 4))])
    to_5 = send(s_1, [((1, 3), (1, 5))])
    p_1, u_1 = solve_first((after(b, s_1), c))
    soon_1, q_1 = subtract(acc, u_1, to_4, to_5)
    a = send(soon_1, [((1, 4), (2, 6)), ((1, 5), (2, 7))])
    b = send(soon_1, [((1, 4), (2, 7)), ((1, 5), (2, 6))])
    got = after(got, soon_1)
    coupling = (got, swap(got))

    outs = [slim] * 2 + [whole] * 2
    one, two, p_2, q_2 = call(
        pair_kernel, "pair", pick("core", "even"), outs, [VMEM] * 8, *inverses, *belows, *coupling, a, b
    )
    a = send(one, [((2, 6), (3, 6)), ((2, 7), (3, 7))])
    b = send(two, [((2, 6), (3, 7)), ((2, 7), (3, 6))])

    late_6 = send(after(q_0, p_1), [((0, 2), (0, 6)), ((0, 3), (0, 7))])
    later = subtract_late(rhs, u, v, after(late_6, soon_1))
    acc = send(later, [((0, c), (1, c)) for c in (6, 7)])
    r_6 = send(after(soon, p_1), [((0, 2), (1, 6))])
    r_7 = send(after(soon, p_1), [((0, 2), (1, 7))])
    to_7 = send(after(s_1, soon_1), [((1, 3), (1, 7))])
    to_6 = send(after(s_1, soon_1), [((1, 3), (1, 6))])
    given = (r_6, r_7, after(to_6, p_2), to_7, acc)
    scalars = pick("core", "even", "six")
    one, two = call(less_kernel, "less", scalars, [slim] * 2, [VMEM] * 9, *inverses, *belows, *given)
    c = send(one, [((1, 6), (3, 6)), ((1, 7), (3, 7))])
    d = send(two, [((1, 6), (3, 7)), ((1, 7), (3, 6))])

    outs = [((2, block // 2, width), F32)]
    known = (after(p_0, one), q_0, p_1, q_1, p_2, q_2)
    (known,) = call(known_kernel, "known", pick("even"), outs, [VMEM] * 6, *known)
    given = (*inverses, *belows, *coupling, after(a, known), b, c, d, known)
    (mine,) = call(final_kernel, "final", pick("core", "even", "own"), outs, [VMEM] * 11, *given)

    cut = block // col_count
    pieces = lax.all_to_all(mine.reshape(col_count, cut, width), "col", 0, 0)
    outs = [((col_count, 2, cut, width), F32)]
    (spread,) = call(spread_kernel, "spread", pick("root"), outs, [VMEM], pieces)
    tile_1 = retile(after(panel, spread), 1)
    other_1 = swap(tile_1)
    pieces = lax.all_to_all(spread, "col", 0, 0)
    outs = [((2, block, width), F32), whole]
    both, theirs = call(gather_kernel, "gather", just_core, outs, [VMEM], pieces)
    theirs = swap(theirs)

    outs = [((row_count, 2, share, width), F32)]
    scalars = pick("core", "keep_p", "keep_q")
    (parts,) = call(update_kernel, "update", scalars, outs, [VMEM] * 5, *belows, tile_1, other_1, both)
    outs = [((1, block, 2 * width), F32)]
    scratch = [pltpu.SemaphoreType.DMA((2,))]
    theirs = after(theirs, parts)
    (solved,) = call(finish_kernel, "finish", just_core, outs, [VMEM] * 2, both, theirs, scratch=scratch, to=ANY)
    parts = lax.all_to_all(after(parts, solved), "row", 0, 0)
    scratch = [pltpu.VMEM((2, share, 2 * width), F32), pltpu.SemaphoreType.DMA((1,))]
    outs = [((2, 1, share, 2 * width), F32)]
    (updated,) = call(combine_kernel, "combine", pick("row"), outs, [VMEM, ANY], parts, right_side, scratch=scratch)
    return solved, updated


def solution(mesh):
    placed = (P(None, "col", None, "row", None), P(None, "col", None, None), P("row", None, None))
    return jax.shard_map(
        shards,
        mesh=mesh,
        in_specs=placed,
        out_specs=(P("row", None, None), P(None, "col", "row", None)),
        check_vma=False,
    )
```

```python
import functools

import jax
import jax.numpy as jnp
from jax import lax
from jax.experimental import pallas as pl
from jax.experimental.pallas import tpu as pltpu
from jax.sharding import PartitionSpec as P

F32 = jnp.float32
BF16 = jnp.bfloat16
LIMIT = 12 * 1024 * 1024
BOTH = ("row", "col")
VMEM = pl.BlockSpec(memory_space=pltpu.VMEM)
SMEM = pl.BlockSpec(memory_space=pltpu.SMEM)
ANY = pl.BlockSpec(memory_space=pl.ANY)


def halves(x):
    hi = x.astype(BF16)
    return hi, (x - hi.astype(F32)).astype(BF16)


def joined(x):
    return jnp.concatenate(halves(x), axis=1)


def product(w, cat):
    n, width = cat.shape[0], cat.shape[1] // 2
    tiles = []
    for i in range(4):
        hi, lo = halves(w(slice(i * n // 4, (i + 1) * n // 4)))
        one = jnp.dot(hi, cat, preferred_element_type=F32)
        two = jnp.dot(lo, cat[:, :width], preferred_element_type=F32)
        tiles.append(one[:, :width] + one[:, width:] + two)
    return jnp.concatenate(tiles, axis=0)


class Pair:
    def __init__(self, ctl, own_ref, other_ref):
        self.first, self.refs = ctl["core"] == 0, (own_ref, other_ref)

    def __getitem__(self, slot):
        def rows(at):
            own, other = (ref[at, :] for ref in self.refs)
            return jnp.where(self.first, own, other) if slot == 0 else jnp.where(self.first, other, own)

        return rows


def packed(x, half):
    n, width = x.shape
    part = x[:, half * width // 2 : (half + 1) * width // 2]
    return jnp.concatenate([part[: n // 2], part[n // 2 :]], axis=1)


def unpacked(x):
    width = x.shape[1] // 2
    return jnp.concatenate([x[:, :width], x[:, width:]], axis=0)


def cost(flops, nbytes):
    return pl.CostEstimate(flops=flops, bytes_accessed=nbytes, transcendentals=0)


class Words:
    def __init__(self, names, refs):
        self.refs = dict(zip(names, refs))

    def __getitem__(self, name):
        return self.refs[name][0]


def call(kernel, name, words, outs, specs, *args, scratch=(), to=VMEM):
    def body(*refs):
        kernel(Words(words, refs), *refs[len(words) :])

    return pl.pallas_call(
        body,
        out_shape=tuple(jax.ShapeDtypeStruct(shape, kind) for shape, kind in outs),
        in_specs=[SMEM] * len(words) + specs,
        out_specs=(to,) * len(outs),
        scratch_shapes=scratch,
        compiler_params=pltpu.CompilerParams(vmem_limit_bytes=LIMIT),
        cost_estimate=cost(0, 0),
        name=name,
    )(*words.values(), *args)


def only(ctl, who, outs, body):
    pl.when(ctl[who] == 1)(body)

    @pl.when(ctl[who] == 0)
    def _():
        for ref in outs:
            ref[...] = jnp.zeros_like(ref)


def after(x, *others):
    return lax.optimization_barrier((x,) + others)[0]


def retile_kernel(a, panel_ref, out_ref, sem):
    copy = pltpu.make_async_copy(panel_ref.at[a, 0, :, 0], out_ref, sem.at[0])
    copy.start()
    copy.wait()


def retile(panel, a):
    n, depth = panel.shape[2], panel.shape[4]
    return pl.pallas_call(
        functools.partial(retile_kernel, a),
        out_shape=jax.ShapeDtypeStruct((n, depth), F32),
        in_specs=[pl.BlockSpec(memory_space=pltpu.HBM)],
        out_specs=VMEM,
        scratch_shapes=[pltpu.SemaphoreType.DMA((1,))],
        compiler_params=pltpu.CompilerParams(vmem_limit_bytes=LIMIT if a else 42 * 1024 * 1024),
        cost_estimate=cost(0, 0),
        name="retile",
    )(panel)


def rhs_kernel(ctl, right_ref, rhs_ref, low_ref, high_ref, sem):
    n, width = rhs_ref.shape
    columns = pl.ds(pl.multiple_of(ctl["column"], width), width)
    copies = [
        pltpu.make_async_copy(right_ref.at[0, 0, rows, columns], ref, sem.at[i])
        for i, (rows, ref) in enumerate(
            ((pl.ds(0, n), rhs_ref), (pl.ds(0, n // 2), low_ref), (pl.ds(n // 2, n // 2), high_ref))
        )
    ]
    for copy in copies:
        copy.start()
    for copy in copies:
        copy.wait()


def cut_kernel(ctl, own_ref, other_ref, out_ref, sem):
    for core, ref in enumerate((own_ref, other_ref)):

        @pl.when((ctl["cut"] == 1) & (ctl["core"] == core))
        def _():
            copy = pltpu.make_async_copy(ref, out_ref, sem.at[0])
            copy.start()
            copy.wait()


def first_kernel(halves_given, ctl, io_ref, ix_ref, lo_ref, lx_ref, *refs):
    parts, s_ref, u_ref = refs[:-2], refs[-2], refs[-1]
    values = [p[...] for p in parts]
    r = jnp.concatenate(values, axis=0) if halves_given else functools.reduce(jnp.add, values)
    s = product(Pair(ctl, io_ref, ix_ref)[0], joined(r))
    s_ref[...] = s
    u_ref[...] = product(Pair(ctl, lo_ref, lx_ref)[0], joined(s))


def follow_kernel(ctl, io_ref, ix_ref, lo_ref, lx_ref, x_ref, y_ref, soon_ref, solved_ref, s_ref, u_ref, mix_ref):
    first_kernel(False, ctl, io_ref, ix_ref, lo_ref, lx_ref, x_ref, y_ref, s_ref, u_ref)
    mix_ref[...] = jnp.where(ctl["zero"] == 1, soon_ref[...], solved_ref[...])


def second_kernel(ctl, io_ref, ix_ref, r_ref, u_ref, s_ref):
    s_ref[...] = product(Pair(ctl, io_ref, ix_ref)[1], joined(r_ref[...] - u_ref[...]))


def third_kernel(ctl, lo_ref, lx_ref, acc_ref, u_ref, x_ref, y_ref, out_ref, sum_ref):
    s = x_ref[...] + y_ref[...]
    sum_ref[...] = s
    out_ref[...] = acc_ref[...] - u_ref[...] - product(Pair(ctl, lo_ref, lx_ref)[1], joined(s))


def later_kernel(ctl, lo_ref, lx_ref, acc_ref, u_ref, v_ref, *refs):
    parts, out_ref = refs[:-1], refs[-1]

    def body():
        s = functools.reduce(jnp.add, [p[...] for p in parts])
        u = u_ref[...] + v_ref[...]
        out_ref[...] = acc_ref[...] - u - product(Pair(ctl, lo_ref, lx_ref)[1], joined(s))

    only(ctl, "late", (out_ref,), body)


def both_ways(even, x, one_ref, two_ref):
    low, high = packed(x, 0), packed(x, 1)
    one_ref[...] = jnp.where(even, low, high)
    two_ref[...] = jnp.where(even, high, low)


def pair_kernel(
    ctl, io_ref, ix_ref, lo_ref, lx_ref, qo_ref, qx_ref, a_ref, b_ref, one_ref, two_ref, p_ref, q_ref
):
    even = ctl["even"] == 1
    inverse, below = Pair(ctl, io_ref, ix_ref), Pair(ctl, lo_ref, lx_ref)
    a, b = a_ref[...], b_ref[...]
    s_p = product(inverse[0], joined(jnp.where(even, a, b)))
    cat = joined(s_p)
    rest = jnp.where(even, b, a) - product(lambda at: qo_ref[at, :] + qx_ref[at, :], cat)
    s_q = product(inverse[1], joined(rest))
    both_ways(even, -product(below[0], cat) - product(below[1], joined(s_q)), one_ref, two_ref)
    p_ref[...] = s_p
    q_ref[...] = s_q


def part_kernel(first, ctl, io_ref, ix_ref, lo_ref, lx_ref, x_ref, acc_ref, *outs):
    below = Pair(ctl, lo_ref, lx_ref)

    def give(value):
        if first:
            outs[0][...] = value
        else:
            both_ways(ctl["even"] == 1, value, *outs)

    @pl.when((ctl["six"] == 1) & (ctl["even"] == first))
    def _():
        give(acc_ref[...] - product(below[1], joined(x_ref[...])))

    @pl.when((ctl["six"] == 1) & (ctl["even"] == 1 - first))
    def _():
        s_p = product(Pair(ctl, io_ref, ix_ref)[0], joined(x_ref[...]))
        give(acc_ref[...] - product(below[0], joined(s_p)))

    @pl.when(ctl["six"] == 0)
    def _():
        for ref in outs:
            ref[...] = jnp.zeros_like(ref)


def known_kernel(ctl, *refs):
    known, out_ref = refs[:-1], refs[-1]
    for slot in range(2):
        s = functools.reduce(jnp.add, [k[...] for k in known[slot::2]])
        out_ref[slot] = jnp.where(ctl["even"] == 1, packed(s, 0), packed(s, 1))


def final_kernel(
    ctl, io_ref, ix_ref, lo_ref, lx_ref, qo_ref, qx_ref, a_ref, b_ref, c_ref, d_ref, known_ref, out_ref
):
    even = ctl["even"] == 1
    inverse, own = Pair(ctl, io_ref, ix_ref), Pair(ctl, lo_ref, lx_ref)[0]

    def coupling(at):
        return jnp.where(ctl["own"] == 1, own(at), qo_ref[at, :] + qx_ref[at, :])

    one, two = a_ref[...] + c_ref[...], b_ref[...] + d_ref[...]
    s_p = product(inverse[0], joined(unpacked(jnp.where(even, one, two))))
    rest = unpacked(jnp.where(even, two, one)) - product(coupling, joined(s_p))
    s_q = product(inverse[1], joined(rest))
    n = s_p.shape[0] // 2
    for slot, s in ((0, s_p), (1, s_q)):
        out_ref[slot] = known_ref[slot] + jnp.concatenate([s[:n], s[n:]], axis=1)


def spread_kernel(ctl, pieces_ref, out_ref):
    piece = pieces_ref[pl.ds(ctl["root"], 2)]
    for j in range(out_ref.shape[0]):
        out_ref[j] = piece


def gather_kernel(ctl, pieces_ref, solved_ref, theirs_ref):
    steps, cuts = pieces_ref.shape[0] // 2, pieces_ref.shape[1]
    for slot in range(2):
        sides = []
        for half in range(cuts):
            pieces = [pieces_ref[slot * steps + j, half] for j in range(steps)]
            sides.append(unpacked(jnp.concatenate(pieces, axis=0)))
        solved_ref[slot] = jnp.concatenate(sides, axis=1)
    theirs_ref[...] = jnp.where(ctl["core"] == 0, solved_ref[1], solved_ref[0])


def update_kernel(ctl, o0_ref, x0_ref, o1_ref, x1_ref, solved_ref, out_ref):
    parts, _, rows, width = out_ref.shape
    cats = [joined(solved_ref[slot]) for slot in range(2)]
    for a, w in enumerate((Pair(ctl, o0_ref, x0_ref), Pair(ctl, o1_ref, x1_ref))):
        terms = [product(w[slot], cats[slot]) for slot in range(2)]
        if a == 0:
            terms = [t * ctl[("keep_p", "keep_q")[slot]].astype(F32) for slot, t in enumerate(terms)]
        total = terms[0] + terms[1]
        for j in range(parts):
            out_ref[j, a] = total[j * rows : (j + 1) * rows]


def finish_kernel(ctl, solved_ref, theirs_ref, out_ref, sem):
    core, width = ctl["core"], theirs_ref.shape[1]
    copies = [
        pltpu.make_async_copy(ref, out_ref.at[0, :, pl.ds(pl.multiple_of(h * width, width), width)], sem.at[i])
        for i, (h, ref) in enumerate(((core, solved_ref.at[core]), (1 - core, theirs_ref)))
    ]
    for copy in copies:
        copy.start()
    for copy in copies:
        copy.wait()


def combine_kernel(ctl, parts_ref, right_ref, out_ref, own_ref, sem):
    share, width = parts_ref.shape[2:]
    rows = pl.ds(pl.multiple_of(ctl["row"], share), share)
    copy = pltpu.make_async_copy(right_ref.at[:, 0, rows, :], own_ref, sem.at[0])
    copy.start()
    sums = [functools.reduce(jnp.add, [parts_ref[2 * z + h] for z in range(parts_ref.shape[0] // 2)]) for h in range(2)]
    copy.wait()
    for h in range(2):
        columns = slice(h * width, (h + 1) * width)
        out_ref[:, 0, :, columns] = own_ref[:, :, columns] - sums[h]


def shards(panel, right_side, inverse_blocks):
    block = panel.shape[2]
    width = right_side.shape[3] // 2
    my_row, my_col = lax.axis_index("row"), lax.axis_index("col")
    row_count, col_count = lax.axis_size("row"), lax.axis_size("col")
    plane, core = my_row // 2, my_row % 2
    share = block // row_count
    whole, half, slim = (((rows, width), F32) for rows in (block, block // 2, block // 2))

    def at(z, low, high):
        return (plane == z) & (my_col >= low) & (my_col <= high)

    words = {
        "core": core,
        "even": my_col % 2 == 0,
        "column": core * width,
        "row": my_row * share,
        "root": jnp.where(plane == 3, 6, 2 * plane + 2),
        "keep_p": my_col > 2 * plane,
        "keep_q": my_col > 2 * plane + 1,
        "own": at(3, 7, 7),
        "cut": at(2, 5, 5) | at(3, 7, 7),
        "zero": plane == 0,
        "late": at(0, 4, 7),
        "six": at(1, 6, 7),
    }
    words = {name: jnp.asarray(word).astype(jnp.int32).reshape(1) for name, word in words.items()}
    panel, right_side, words = lax.optimization_barrier((panel, right_side, words))

    def pick(*names):
        return {name: words[name] for name in names}

    just_core = pick("core")

    def permute(array, moves):
        place = [[(2 * z + h) * col_count + c for z, h, c in ends] for ends in moves]
        return lax.ppermute(array, BOTH, [tuple(p) for p in place])

    def send(array, moves):
        return permute(array, [((a, h, b), (c, h, d)) for (a, b), (c, d) in moves for h in range(2)])

    def swap(array):
        return lax.ppermute(array, "row", [(r, r ^ 1) for r in range(row_count)])

    inverse = inverse_blocks[0]
    tile = retile(panel, 0)
    belows = (tile, swap(tile))
    inverses = (inverse, swap(inverse))
    scratch = [pltpu.SemaphoreType.DMA((3,))]
    outs = [whole, half, half]
    rhs, low, high = call(rhs_kernel, "rhs", pick("column"), outs, [ANY], after(right_side, tile), scratch=scratch)
    low_1 = send(low, [((0, 0), (0, 1)), ((1, 0), (0, 2)), ((3, 0), (0, 3)), ((2, 0), (0, 4))])
    high_1 = send(high, [((3, 0), (0, 1)), ((0, 0), (0, 2)), ((1, 0), (0, 3)), ((2, 0), (0, 4))])

    def solve_first(parts, halves_given=False):
        kernel = functools.partial(first_kernel, halves_given)
        return call(kernel, "first", just_core, [whole] * 2, [VMEM] * (4 + len(parts)), *inverses, *belows, *parts)

    def solve_second(r, u):
        return call(second_kernel, "second", just_core, [whole], [VMEM] * 4, *inverses, r, u)[0]

    def subtract(acc, u, x, y):
        return call(third_kernel, "third", just_core, [whole] * 2, [VMEM] * 6, *belows, acc, u, x, y)

    def subtract_late(acc, u, v, *parts):
        specs = [VMEM] * (5 + len(parts))
        return call(later_kernel, "later", pick("core", "late"), [whole], specs, *belows, acc, u, v, *parts)[0]

    p_0, u = solve_first((low_1, high_1), True)
    s_q = solve_second(rhs, u)
    to_2 = send(s_q, [((0, 1), (0, 2))])
    to_3 = send(s_q, [((0, 1), (0, 3))])
    low_2 = send(after(low, low_1), [((0, 0), (0, 5)), ((1, 0), (0, 6)), ((3, 0), (0, 7))])
    high_2 = send(after(high, low_1), [((1, 0), (0, 5)), ((3, 0), (0, 6)), ((0, 0), (0, 7))])
    _, v = solve_first((after(low_2, s_q), high_2), True)

    soon, q_0 = subtract(rhs, u, to_2, to_3)
    a = send(soon, [((0, 2), (1, 3))])
    b = send(soon, [((0, 3), (1, 3)), ((0, 2), (1, 4))])
    c = send(soon, [((0, 2), (1, 5))])

    late_5 = send(s_q, [((0, 1), (0, 5))])
    late_4 = send(s_q, [((0, 1), (0, 4))])
    later = subtract_late(rhs, u, v, after(late_5, soon), late_4)
    acc = send(later, [((0, c), (1, c)) for c in (4, 5)])

    outs = [((block, block), F32)]
    scratch = [pltpu.SemaphoreType.DMA((1,))]
    given = (tile, after(belows[1], later))
    (ahead,) = call(cut_kernel, "cut", pick("core", "cut"), outs, [ANY] * 2, *given, scratch=scratch)
    got = permute(ahead, [((2, 0, 5), (2, 0, 6)), ((2, 1, 5), (2, 1, 7)), ((3, 0, 7), (3, 0, 6))])

    tile_1 = retile(after(panel, a), 1)
    _, u_1 = solve_first((after(a, later, tile_1),))
    s_1 = solve_second(b, u_1)
    to_4 = send(s_1, [((1, 3), (1, 4))])
    to_5 = send(s_1, [((1, 3), (1, 5))])
    given = (*inverses, *belows, after(b, s_1), c, soon, s_1)
    p_1, u_1, mix = call(follow_kernel, "follow", pick("core", "zero"), [whole] * 3, [VMEM] * 8, *given)
    soon_1, q_1 = subtract(acc, u_1, to_4, to_5)
    a = send(soon_1, [((1, 4), (2, 6)), ((1, 5), (2, 7))])
    b = send(soon_1, [((1, 4), (2, 7)), ((1, 5), (2, 6))])
    got = after(got, soon_1)
    coupling = (got, swap(got))

    outs = [slim] * 2 + [whole] * 2
    one, two, p_2, q_2 = call(
        pair_kernel, "pair", pick("core", "even"), outs, [VMEM] * 8, *inverses, *belows, *coupling, a, b
    )
    a = send(one, [((2, 6), (3, 6)), ((2, 7), (3, 7))])
    b = send(two, [((2, 6), (3, 7)), ((2, 7), (3, 6))])

    late_6 = send(after(q_0, p_1), [((0, 2), (0, 6)), ((0, 3), (0, 7))])
    later = subtract_late(rhs, u, v, after(late_6, soon_1))
    acc = send(later, [((0, c), (1, c)) for c in (6, 7)])
    mix = after(mix, soon_1)
    one_way = send(mix, [((0, 2), (1, 6)), ((1, 3), (1, 7))])
    other_way = send(mix, [((0, 2), (1, 7)), ((1, 3), (1, 6))])
    scalars = pick("core", "even", "six")
    blocks = (*inverses, *belows)
    kernel = functools.partial(part_kernel, 1)
    (less,) = call(kernel, "less", scalars, [whole], [VMEM] * 6, *blocks, after(other_way, p_2), acc)
    kernel = functools.partial(part_kernel, 0)
    one, two = call(kernel, "less", scalars, [slim] * 2, [VMEM] * 6, *blocks, one_way, less)
    c = send(one, [((1, 6), (3, 6)), ((1, 7), (3, 7))])
    d = send(two, [((1, 6), (3, 7)), ((1, 7), (3, 6))])

    outs = [((2, block // 2, width), F32)]
    known = (after(p_0, one), q_0, p_1, q_1, p_2, q_2)
    (known,) = call(known_kernel, "known", pick("even"), outs, [VMEM] * 6, *known)
    other_1 = swap(after(tile_1, known))
    given = (*inverses, *belows, *coupling, after(a, known), b, c, d, known)
    (mine,) = call(final_kernel, "final", pick("core", "even", "own"), outs, [VMEM] * 11, *given)

    cut = block // col_count
    pieces = lax.all_to_all(mine.reshape(col_count, cut, width), "col", 0, 0)
    outs = [((col_count, 2, cut, width), F32)]
    (spread,) = call(spread_kernel, "spread", pick("root"), outs, [VMEM], pieces)
    pieces = lax.all_to_all(spread, "col", 0, 0)
    outs = [((2, block, width), F32), whole]
    both, theirs = call(gather_kernel, "gather", just_core, outs, [VMEM], pieces)
    theirs = swap(theirs)

    outs = [((row_count, 2, share, width), F32)]
    scalars = pick("core", "keep_p", "keep_q")
    (parts,) = call(update_kernel, "update", scalars, outs, [VMEM] * 5, *belows, tile_1, other_1, both)
    outs = [((1, block, 2 * width), F32)]
    scratch = [pltpu.SemaphoreType.DMA((2,))]
    theirs = after(theirs, parts)
    (solved,) = call(finish_kernel, "finish", just_core, outs, [VMEM] * 2, both, theirs, scratch=scratch, to=ANY)
    parts = lax.all_to_all(after(parts, solved), "row", 0, 0)
    scratch = [pltpu.VMEM((2, share, 2 * width), F32), pltpu.SemaphoreType.DMA((1,))]
    outs = [((2, 1, share, 2 * width), F32)]
    (updated,) = call(combine_kernel, "combine", pick("row"), outs, [VMEM, ANY], parts, right_side, scratch=scratch)
    return solved, updated


def solution(mesh):
    placed = (P(None, "col", None, "row", None), P(None, "col", None, None), P("row", None, None))
    return jax.shard_map(
        shards,
        mesh=mesh,
        in_specs=placed,
        out_specs=(P("row", None, None), P(None, "col", "row", None)),
        check_vma=False,
    )
```

```python
import functools

import jax
import jax.numpy as jnp
from jax import lax
from jax.experimental import pallas as pl
from jax.experimental.pallas import tpu as pltpu
from jax.sharding import PartitionSpec as P

F32 = jnp.float32
BF16 = jnp.bfloat16
LIMIT = 12 * 1024 * 1024
BOTH = ("row", "col")
VMEM = pl.BlockSpec(memory_space=pltpu.VMEM)
SMEM = pl.BlockSpec(memory_space=pltpu.SMEM)
ANY = pl.BlockSpec(memory_space=pl.ANY)


def halves(x):
    hi = x.astype(BF16)
    return hi, (x - hi.astype(F32)).astype(BF16)


def joined(x):
    return jnp.concatenate(halves(x), axis=1)


def product(w, cat):
    n, width = cat.shape[0], cat.shape[1] // 2
    tiles = []
    for i in range(4):
        hi, lo = halves(w(slice(i * n // 4, (i + 1) * n // 4)))
        one = jnp.dot(hi, cat, preferred_element_type=F32)
        two = jnp.dot(lo, cat[:, :width], preferred_element_type=F32)
        tiles.append(one[:, :width] + one[:, width:] + two)
    return jnp.concatenate(tiles, axis=0)


class Pair:
    def __init__(self, ctl, own_ref, other_ref):
        self.first, self.refs = ctl["core"] == 0, (own_ref, other_ref)

    def __getitem__(self, slot):
        def rows(at):
            own, other = (ref[at, :] for ref in self.refs)
            return jnp.where(self.first, own, other) if slot == 0 else jnp.where(self.first, other, own)

        return rows


def packed(x, half):
    n, width = x.shape
    part = x[:, half * width // 2 : (half + 1) * width // 2]
    return jnp.concatenate([part[: n // 2], part[n // 2 :]], axis=1)


def unpacked(x):
    width = x.shape[1] // 2
    return jnp.concatenate([x[:, :width], x[:, width:]], axis=0)


def cost(flops, nbytes):
    return pl.CostEstimate(flops=flops, bytes_accessed=nbytes, transcendentals=0)


class Words:
    def __init__(self, names, refs):
        self.refs = dict(zip(names, refs))

    def __getitem__(self, name):
        return self.refs[name][0]


def call(kernel, name, words, outs, specs, *args, scratch=(), to=VMEM):
    def body(*refs):
        kernel(Words(words, refs), *refs[len(words) :])

    return pl.pallas_call(
        body,
        out_shape=tuple(jax.ShapeDtypeStruct(shape, kind) for shape, kind in outs),
        in_specs=[SMEM] * len(words) + specs,
        out_specs=(to,) * len(outs),
        scratch_shapes=scratch,
        compiler_params=pltpu.CompilerParams(vmem_limit_bytes=LIMIT),
        cost_estimate=cost(0, 0),
        name=name,
    )(*words.values(), *args)


def only(ctl, who, outs, body):
    pl.when(ctl[who] == 1)(body)

    @pl.when(ctl[who] == 0)
    def _():
        for ref in outs:
            ref[...] = jnp.zeros_like(ref)


def after(x, *others):
    return lax.optimization_barrier((x,) + others)[0]


def retile_kernel(a, panel_ref, out_ref, sem):
    copy = pltpu.make_async_copy(panel_ref.at[a, 0, :, 0], out_ref, sem.at[0])
    copy.start()
    copy.wait()


def retile(panel, a):
    n, depth = panel.shape[2], panel.shape[4]
    return pl.pallas_call(
        functools.partial(retile_kernel, a),
        out_shape=jax.ShapeDtypeStruct((n, depth), F32),
        in_specs=[pl.BlockSpec(memory_space=pltpu.HBM)],
        out_specs=VMEM,
        scratch_shapes=[pltpu.SemaphoreType.DMA((1,))],
        compiler_params=pltpu.CompilerParams(vmem_limit_bytes=LIMIT if a else 42 * 1024 * 1024),
        cost_estimate=cost(0, 0),
        name="retile",
    )(panel)


def rhs_kernel(ctl, right_ref, rhs_ref, low_ref, high_ref, sem):
    n, width = rhs_ref.shape
    columns = pl.ds(pl.multiple_of(ctl["column"], width), width)
    copies = [
        pltpu.make_async_copy(right_ref.at[0, 0, rows, columns], ref, sem.at[i])
        for i, (rows, ref) in enumerate(
            ((pl.ds(0, n), rhs_ref), (pl.ds(0, n // 2), low_ref), (pl.ds(n // 2, n // 2), high_ref))
        )
    ]
    for copy in copies:
        copy.start()
    for copy in copies:
        copy.wait()


def cut_kernel(ctl, own_ref, other_ref, out_ref, sem):
    for core, ref in enumerate((own_ref, other_ref)):

        @pl.when((ctl["cut"] == 1) & (ctl["core"] == core))
        def _():
            copy = pltpu.make_async_copy(ref, out_ref, sem.at[0])
            copy.start()
            copy.wait()


def first_kernel(halves_given, ctl, io_ref, ix_ref, lo_ref, lx_ref, *refs):
    parts, s_ref, u_ref = refs[:-2], refs[-2], refs[-1]
    values = [p[...] for p in parts]
    r = jnp.concatenate(values, axis=0) if halves_given else functools.reduce(jnp.add, values)
    s = product(Pair(ctl, io_ref, ix_ref)[0], joined(r))
    s_ref[...] = s
    u_ref[...] = product(Pair(ctl, lo_ref, lx_ref)[0], joined(s))


def follow_kernel(ctl, io_ref, ix_ref, lo_ref, lx_ref, x_ref, y_ref, soon_ref, solved_ref, s_ref, u_ref, mix_ref):
    first_kernel(False, ctl, io_ref, ix_ref, lo_ref, lx_ref, x_ref, y_ref, s_ref, u_ref)
    mix_ref[...] = jnp.where(ctl["zero"] == 1, soon_ref[...], solved_ref[...])


def second_kernel(ctl, io_ref, ix_ref, r_ref, u_ref, s_ref):
    s_ref[...] = product(Pair(ctl, io_ref, ix_ref)[1], joined(r_ref[...] - u_ref[...]))


def third_kernel(ctl, lo_ref, lx_ref, acc_ref, u_ref, x_ref, y_ref, out_ref, sum_ref):
    s = x_ref[...] + y_ref[...]
    sum_ref[...] = s
    out_ref[...] = acc_ref[...] - u_ref[...] - product(Pair(ctl, lo_ref, lx_ref)[1], joined(s))


def fourth_kernel(ctl, lo_ref, lx_ref, acc_ref, u_ref, x_ref, y_ref, out_ref, sum_ref):
    def body():
        third_kernel(ctl, lo_ref, lx_ref, acc_ref, u_ref, x_ref, y_ref, out_ref, sum_ref)

    only(ctl, "four", (out_ref, sum_ref), body)


def later_kernel(ctl, lo_ref, lx_ref, acc_ref, u_ref, v_ref, *refs):
    parts, out_ref = refs[:-1], refs[-1]

    def body():
        s = functools.reduce(jnp.add, [p[...] for p in parts])
        u = u_ref[...] + v_ref[...]
        out_ref[...] = acc_ref[...] - u - product(Pair(ctl, lo_ref, lx_ref)[1], joined(s))

    only(ctl, "late", (out_ref,), body)


def both_ways(even, x, one_ref, two_ref):
    low, high = packed(x, 0), packed(x, 1)
    one_ref[...] = jnp.where(even, low, high)
    two_ref[...] = jnp.where(even, high, low)


def pair_kernel(
    ctl, io_ref, ix_ref, lo_ref, lx_ref, qo_ref, qx_ref, a_ref, b_ref, one_ref, two_ref, p_ref, q_ref
):
    even = ctl["even"] == 1
    inverse, below = Pair(ctl, io_ref, ix_ref), Pair(ctl, lo_ref, lx_ref)
    a, b = a_ref[...], b_ref[...]
    s_p = product(inverse[0], joined(jnp.where(even, a, b)))
    cat = joined(s_p)
    rest = jnp.where(even, b, a) - product(lambda at: qo_ref[at, :] + qx_ref[at, :], cat)
    s_q = product(inverse[1], joined(rest))
    both_ways(even, -product(below[0], cat) - product(below[1], joined(s_q)), one_ref, two_ref)
    p_ref[...] = s_p
    q_ref[...] = s_q


def part_kernel(first, ctl, io_ref, ix_ref, lo_ref, lx_ref, x_ref, acc_ref, *outs):
    below = Pair(ctl, lo_ref, lx_ref)

    def give(value):
        if first:
            outs[0][...] = value
        else:
            both_ways(ctl["even"] == 1, value, *outs)

    @pl.when((ctl["six"] == 1) & (ctl["even"] == first))
    def _():
        give(acc_ref[...] - product(below[1], joined(x_ref[...])))

    @pl.when((ctl["six"] == 1) & (ctl["even"] == 1 - first))
    def _():
        s_p = product(Pair(ctl, io_ref, ix_ref)[0], joined(x_ref[...]))
        give(acc_ref[...] - product(below[0], joined(s_p)))

    @pl.when(ctl["six"] == 0)
    def _():
        for ref in outs:
            ref[...] = jnp.zeros_like(ref)


def known_kernel(ctl, *refs):
    known, out_ref = refs[:-1], refs[-1]
    for slot in range(2):
        s = functools.reduce(jnp.add, [k[...] for k in known[slot::2]])
        out_ref[slot] = jnp.where(ctl["even"] == 1, packed(s, 0), packed(s, 1))


def final_kernel(
    ctl, io_ref, ix_ref, lo_ref, lx_ref, qo_ref, qx_ref, a_ref, b_ref, c_ref, d_ref, known_ref, out_ref
):
    even = ctl["even"] == 1
    inverse, own = Pair(ctl, io_ref, ix_ref), Pair(ctl, lo_ref, lx_ref)[0]

    def coupling(at):
        return jnp.where(ctl["own"] == 1, own(at), qo_ref[at, :] + qx_ref[at, :])

    one, two = a_ref[...] + c_ref[...], b_ref[...] + d_ref[...]
    s_p = product(inverse[0], joined(unpacked(jnp.where(even, one, two))))
    rest = unpacked(jnp.where(even, two, one)) - product(coupling, joined(s_p))
    s_q = product(inverse[1], joined(rest))
    n = s_p.shape[0] // 2
    for slot, s in ((0, s_p), (1, s_q)):
        out_ref[slot] = known_ref[slot] + jnp.concatenate([s[:n], s[n:]], axis=1)


def spread_kernel(ctl, pieces_ref, out_ref):
    piece = pieces_ref[pl.ds(ctl["root"], 2)]
    for j in range(out_ref.shape[0]):
        out_ref[j] = piece


def gather_kernel(ctl, pieces_ref, solved_ref, theirs_ref):
    steps, cuts = pieces_ref.shape[0] // 2, pieces_ref.shape[1]
    for slot in range(2):
        sides = []
        for half in range(cuts):
            pieces = [pieces_ref[slot * steps + j, half] for j in range(steps)]
            sides.append(unpacked(jnp.concatenate(pieces, axis=0)))
        solved_ref[slot] = jnp.concatenate(sides, axis=1)
    theirs_ref[...] = jnp.where(ctl["core"] == 0, solved_ref[1], solved_ref[0])


def update_kernel(ctl, o0_ref, x0_ref, o1_ref, x1_ref, solved_ref, out_ref):
    parts, _, rows, width = out_ref.shape
    cats = [joined(solved_ref[slot]) for slot in range(2)]
    for a, w in enumerate((Pair(ctl, o0_ref, x0_ref), Pair(ctl, o1_ref, x1_ref))):
        terms = [product(w[slot], cats[slot]) for slot in range(2)]
        if a == 0:
            terms = [t * ctl[("keep_p", "keep_q")[slot]].astype(F32) for slot, t in enumerate(terms)]
        total = terms[0] + terms[1]
        for j in range(parts):
            out_ref[j, a] = total[j * rows : (j + 1) * rows]


def finish_kernel(ctl, solved_ref, theirs_ref, out_ref, sem):
    core, width = ctl["core"], theirs_ref.shape[1]
    copies = [
        pltpu.make_async_copy(ref, out_ref.at[0, :, pl.ds(pl.multiple_of(h * width, width), width)], sem.at[i])
        for i, (h, ref) in enumerate(((core, solved_ref.at[core]), (1 - core, theirs_ref)))
    ]
    for copy in copies:
        copy.start()
    for copy in copies:
        copy.wait()


def combine_kernel(ctl, parts_ref, right_ref, out_ref, own_ref, sem):
    share, width = parts_ref.shape[2:]
    rows = pl.ds(pl.multiple_of(ctl["row"], share), share)
    copy = pltpu.make_async_copy(right_ref.at[:, 0, rows, :], own_ref, sem.at[0])
    copy.start()
    sums = [functools.reduce(jnp.add, [parts_ref[2 * z + h] for z in range(parts_ref.shape[0] // 2)]) for h in range(2)]
    copy.wait()
    for h in range(2):
        columns = slice(h * width, (h + 1) * width)
        out_ref[:, 0, :, columns] = own_ref[:, :, columns] - sums[h]


def shards(panel, right_side, inverse_blocks):
    block = panel.shape[2]
    width = right_side.shape[3] // 2
    my_row, my_col = lax.axis_index("row"), lax.axis_index("col")
    row_count, col_count = lax.axis_size("row"), lax.axis_size("col")
    plane, core = my_row // 2, my_row % 2
    share = block // row_count
    whole, half, slim = (((rows, width), F32) for rows in (block, block // 2, block // 2))

    def at(z, low, high):
        return (plane == z) & (my_col >= low) & (my_col <= high)

    words = {
        "core": core,
        "even": my_col % 2 == 0,
        "column": core * width,
        "row": my_row * share,
        "root": jnp.where(plane == 3, 6, 2 * plane + 2),
        "keep_p": my_col > 2 * plane,
        "keep_q": my_col > 2 * plane + 1,
        "own": at(3, 7, 7),
        "cut": at(2, 5, 5) | at(3, 7, 7),
        "zero": plane == 0,
        "late": at(0, 4, 7),
        "four": at(1, 4, 5),
        "six": at(1, 6, 7),
    }
    words = {name: jnp.asarray(word).astype(jnp.int32).reshape(1) for name, word in words.items()}
    panel, right_side, words = lax.optimization_barrier((panel, right_side, words))

    def pick(*names):
        return {name: words[name] for name in names}

    just_core = pick("core")

    def permute(array, moves):
        place = [[(2 * z + h) * col_count + c for z, h, c in ends] for ends in moves]
        return lax.ppermute(array, BOTH, [tuple(p) for p in place])

    def send(array, moves):
        return permute(array, [((a, h, b), (c, h, d)) for (a, b), (c, d) in moves for h in range(2)])

    def swap(array):
        return lax.ppermute(array, "row", [(r, r ^ 1) for r in range(row_count)])

    inverse = inverse_blocks[0]
    tile = retile(panel, 0)
    belows = (tile, swap(tile))
    inverses = (inverse, swap(inverse))
    scratch = [pltpu.SemaphoreType.DMA((3,))]
    outs = [whole, half, half]
    rhs, low, high = call(rhs_kernel, "rhs", pick("column"), outs, [ANY], after(right_side, tile), scratch=scratch)
    low_1 = send(low, [((0, 0), (0, 1)), ((1, 0), (0, 2)), ((3, 0), (0, 3)), ((2, 0), (0, 4))])
    high_1 = send(high, [((3, 0), (0, 1)), ((0, 0), (0, 2)), ((1, 0), (0, 3)), ((2, 0), (0, 4))])

    def solve_first(parts, halves_given=False):
        kernel = functools.partial(first_kernel, halves_given)
        return call(kernel, "first", just_core, [whole] * 2, [VMEM] * (4 + len(parts)), *inverses, *belows, *parts)

    def solve_second(r, u):
        return call(second_kernel, "second", just_core, [whole], [VMEM] * 4, *inverses, r, u)[0]

    def subtract(acc, u, x, y):
        return call(third_kernel, "third", just_core, [whole] * 2, [VMEM] * 6, *belows, acc, u, x, y)

    def subtract_late(acc, u, v, *parts):
        specs = [VMEM] * (5 + len(parts))
        return call(later_kernel, "later", pick("core", "late"), [whole], specs, *belows, acc, u, v, *parts)[0]

    p_0, u = solve_first((low_1, high_1), True)
    s_q = solve_second(rhs, u)
    to_2 = send(s_q, [((0, 1), (0, 2))])
    to_3 = send(s_q, [((0, 1), (0, 3))])
    low_2 = send(after(low, low_1), [((0, 0), (0, 5)), ((1, 0), (0, 6)), ((3, 0), (0, 7))])
    high_2 = send(after(high, low_1), [((1, 0), (0, 5)), ((3, 0), (0, 6)), ((0, 0), (0, 7))])
    _, v = solve_first((after(low_2, s_q), high_2), True)

    soon, q_0 = subtract(rhs, u, to_2, to_3)
    a = send(soon, [((0, 2), (1, 3))])
    b = send(soon, [((0, 3), (1, 3)), ((0, 2), (1, 4))])
    c = send(soon, [((0, 2), (1, 5))])

    late_5 = send(s_q, [((0, 1), (0, 5))])
    late_4 = send(s_q, [((0, 1), (0, 4))])
    later = subtract_late(rhs, u, v, after(late_5, soon), late_4)
    acc = send(later, [((0, c), (1, c)) for c in (4, 5)])

    outs = [((block, block), F32)]
    scratch = [pltpu.SemaphoreType.DMA((1,))]
    given = (tile, after(belows[1], later))
    (ahead,) = call(cut_kernel, "cut", pick("core", "cut"), outs, [ANY] * 2, *given, scratch=scratch)
    got = permute(ahead, [((2, 0, 5), (2, 0, 6)), ((2, 1, 5), (2, 1, 7)), ((3, 0, 7), (3, 0, 6))])

    tile_1 = retile(after(panel, a), 1)
    _, u_1 = solve_first((after(a, later, tile_1),))
    s_1 = solve_second(b, u_1)
    to_4 = send(s_1, [((1, 3), (1, 4))])
    to_5 = send(s_1, [((1, 3), (1, 5))])
    given = (*inverses, *belows, after(b, s_1), c, soon, s_1)
    p_1, u_1, mix = call(follow_kernel, "follow", pick("core", "zero"), [whole] * 3, [VMEM] * 8, *given)
    given = (*belows, acc, u_1, to_4, to_5)
    soon_1, q_1 = call(fourth_kernel, "third", pick("core", "four"), [whole] * 2, [VMEM] * 6, *given)
    a = send(soon_1, [((1, 4), (2, 6)), ((1, 5), (2, 7))])
    b = send(soon_1, [((1, 4), (2, 7)), ((1, 5), (2, 6))])
    got = after(got, soon_1)
    coupling = (got, swap(got))

    outs = [slim] * 2 + [whole] * 2
    one, two, p_2, q_2 = call(
        pair_kernel, "pair", pick("core", "even"), outs, [VMEM] * 8, *inverses, *belows, *coupling, a, b
    )
    a = send(one, [((2, 6), (3, 6)), ((2, 7), (3, 7))])
    b = send(two, [((2, 6), (3, 7)), ((2, 7), (3, 6))])

    late_6 = send(after(q_0, p_1), [((0, 2), (0, 6)), ((0, 3), (0, 7))])
    later = subtract_late(rhs, u, v, after(late_6, soon_1))
    acc = send(later, [((0, c), (1, c)) for c in (6, 7)])
    mix = after(mix, soon_1)
    one_way = send(mix, [((0, 2), (1, 6)), ((1, 3), (1, 7))])
    other_way = send(mix, [((0, 2), (1, 7)), ((1, 3), (1, 6))])
    scalars = pick("core", "even", "six")
    blocks = (*inverses, *belows)
    kernel = functools.partial(part_kernel, 1)
    (less,) = call(kernel, "less", scalars, [whole], [VMEM] * 6, *blocks, after(other_way, p_2), acc)
    kernel = functools.partial(part_kernel, 0)
    one, two = call(kernel, "less", scalars, [slim] * 2, [VMEM] * 6, *blocks, one_way, less)
    c = send(one, [((1, 6), (3, 6)), ((1, 7), (3, 7))])
    d = send(two, [((1, 6), (3, 7)), ((1, 7), (3, 6))])

    outs = [((2, block // 2, width), F32)]
    known = (after(p_0, one), q_0, p_1, q_1, p_2, q_2)
    (known,) = call(known_kernel, "known", pick("even"), outs, [VMEM] * 6, *known)
    other_1 = swap(after(tile_1, known))
    given = (*inverses, *belows, *coupling, after(a, known), b, c, d, known)
    (mine,) = call(final_kernel, "final", pick("core", "even", "own"), outs, [VMEM] * 11, *given)

    cut = block // col_count
    pieces = lax.all_to_all(mine.reshape(col_count, cut, width), "col", 0, 0)
    outs = [((col_count, 2, cut, width), F32)]
    (spread,) = call(spread_kernel, "spread", pick("root"), outs, [VMEM], pieces)
    pieces = lax.all_to_all(spread, "col", 0, 0)
    outs = [((2, block, width), F32), whole]
    both, theirs = call(gather_kernel, "gather", just_core, outs, [VMEM], pieces)
    theirs = swap(theirs)

    outs = [((row_count, 2, share, width), F32)]
    scalars = pick("core", "keep_p", "keep_q")
    (parts,) = call(update_kernel, "update", scalars, outs, [VMEM] * 5, *belows, tile_1, other_1, both)
    outs = [((1, block, 2 * width), F32)]
    scratch = [pltpu.SemaphoreType.DMA((2,))]
    theirs = after(theirs, parts)
    (solved,) = call(finish_kernel, "finish", just_core, outs, [VMEM] * 2, both, theirs, scratch=scratch, to=ANY)
    parts = lax.all_to_all(after(parts, solved), "row", 0, 0)
    scratch = [pltpu.VMEM((2, share, 2 * width), F32), pltpu.SemaphoreType.DMA((1,))]
    outs = [((2, 1, share, 2 * width), F32)]
    (updated,) = call(combine_kernel, "combine", pick("row"), outs, [VMEM, ANY], parts, right_side, scratch=scratch)
    return solved, updated


def solution(mesh):
    placed = (P(None, "col", None, "row", None), P(None, "col", None, None), P("row", None, None))
    return jax.shard_map(
        shards,
        mesh=mesh,
        in_specs=placed,
        out_specs=(P("row", None, None), P(None, "col", "row", None)),
        check_vma=False,
    )
```
